512 devices in a mesh: section: 32 (over x, z_lo, core), tile: 16 (over z_hi, y).
Axes of the slice: x: 4, y: 8, z: 8 (z_hi: 2, z_lo: 4; z = z_hi * 4 + z_lo), core: 2. Of those that a mesh axis runs over, the one named last changes fastest.
Arguments:
- saved_inputs: bfloat16 [32, 4, 256, 32, 256], P('section', None, 'tile'), may hold values from -6 to 6
- relu_mask: int32 [32, 4, 256, 32, 256], P('section', None, 'tile'), may hold values from 0 to 1
- grads_in: bfloat16 [32, 256, 32, 256], P('section', 'tile'), may hold values from -6 to 6
- head_grads: bfloat16 [3, 256, 32, 256], P(None, 'tile'), may hold values from -6 to 6
- kernels: bfloat16 [32, 3, 3, 256, 256], P('section'), may hold values from -0.125 to 0.125
- bn_scale: float32 [32, 256], P('section'), may hold values from 0.5 to 2
Outputs:
- kernel_grads: float32 [32, 2304, 256], P('section', 'tile')
- outgoing: bfloat16 [32, 256, 32, 256], P('section', 'tile')
The draws below stay inside these ranges and needn't reach their ends.
All inputs are finite; a program needn't handle non-finite values.
Results may differ from the reference program's by a relative error of at most 0.019.
Values may be sent and summed in bfloat16 or wider, within the bound.
A program may use at most 64 MiB of HBM per device.

```python
import math
import jax
import jax.numpy as jnp
from jax import lax

CH = 256
IMG_W = 32
TICKS = 4
SECTIONS = 32
IMG_H = 256


def with_ends(result, key, smallest, top_value):
    index_at = [jax.random.randint(jax.random.fold_in(key, axis), (), 0, length) for axis, length in enumerate(result.shape)]
    widest = result.shape.index(max(result.shape))
    beside = index_at[:widest] + [(index_at[widest] + 1) % result.shape[widest]] + index_at[widest + 1:]
    return result.at[tuple(index_at)].set(smallest).at[tuple(beside)].set(top_value)


def block_levels(key, shape, split, smallest, largest):
    gain, own = 1.0, jax.random.fold_in(key, 6)
    for axis_at, parts in split:
        draws = jnp.exp(jax.random.uniform(jax.random.fold_in(own, axis_at), (parts,), jnp.float32, smallest / len(split), largest / len(split)))
        gain = gain * jnp.repeat(draws, shape[axis_at] // parts).reshape([-1 if axis == axis_at else 1 for axis in range(len(shape))])
    return gain


def gaussian(rng, dims, spread, reach, cuts=(), held_as=jnp.bfloat16):
    values = spread * jax.random.normal(rng, dims, jnp.float32)
    if cuts:
        values = values * block_levels(rng, dims, cuts, -0.22, 0.18)
    return jnp.clip(values, -reach, reach).astype(held_as)


def setup_inputs(seed: int = 0) -> dict:
    key_of = jax.random.split(jax.random.key(seed), 7)
    saved_inputs = gaussian(key_of[0], (SECTIONS, TICKS, IMG_H, IMG_W, CH), 1.0, 6.0, ((0, 32), (2, 16)))
    relu_mask = with_ends(jax.random.randint(key_of[1], (SECTIONS, TICKS, IMG_H, IMG_W, CH), 0, 2), jax.random.fold_in(key_of[1], 1), 0, 1).astype(jnp.int32)
    grads_in = gaussian(key_of[2], (SECTIONS, IMG_H, IMG_W, CH), 1.0, 6.0, ((0, 32), (1, 16)))
    head_grads = gaussian(key_of[3], (TICKS - 1, IMG_H, IMG_W, CH), 1.0, 6.0, ((1, 16),))
    kernels = gaussian(key_of[4], (SECTIONS, 3, 3, CH, CH), (9 * CH) ** -0.5, 0.125, ((0, 32),))
    bn_scale = jnp.clip(jnp.exp(math.log(2.0) - 1.3862944 * jax.random.uniform(key_of[5], (SECTIONS, CH), jnp.float32) ** block_levels(key_of[5], (SECTIONS, CH), ((0, 32),), -0.2, 0.2)), 0.5, 2.0)
    return {"saved_inputs": saved_inputs, "relu_mask": relu_mask, "grads_in": grads_in, "head_grads": head_grads, "kernels": kernels, "bn_scale": bn_scale}


def windows(padded, height, columns):
    pieces = [padded[a:a + height, b:b + columns] for a in range(3) for b in range(3)]
    joined = jnp.concatenate(pieces, axis=-1)
    return joined.reshape(height * columns, -1)

def section_back(saved, gate_bits, gradient, kernel, scales):
    channels = saved.shape[-1]
    padded_in = jnp.pad(saved, ((1, 1), (1, 1), (0, 0)))
    input_windows = windows(padded_in, IMG_H, IMG_W)
    pre_grad = (gradient.astype(jnp.float32) * gate_bits.astype(jnp.float32) * scales).astype(jnp.bfloat16)
    padded_grad = jnp.pad(pre_grad, ((1, 1), (1, 1), (0, 0)))
    flipped = kernel[::-1, ::-1].transpose(0, 1, 3, 2).reshape(9 * channels, channels)
    back_grad = jnp.dot(windows(padded_grad, IMG_H, IMG_W), flipped, preferred_element_type=jnp.float32)
    back_grad = back_grad.astype(jnp.bfloat16).reshape(IMG_H, IMG_W, channels)
    kernel_part = lax.dot_general(input_windows, pre_grad.reshape(-1, channels), (((0,), (0,)), ((), ())), preferred_element_type=jnp.float32)
    return (back_grad, kernel_part)

def reference(saved_inputs, relu_mask, grads_in, head_grads, kernels, bn_scale):
    gradient = grads_in
    kernel_total = jnp.zeros((SECTIONS, 9 * CH, CH), jnp.float32)
    back_grad = grads_in
    for tick in range(TICKS):
        back_grad, kernel_part = lax.map(lambda items: section_back(*items), (saved_inputs[:, tick], relu_mask[:, tick], gradient, kernels, bn_scale))
        kernel_total = kernel_total + kernel_part
        if tick + 1 < TICKS:
            gradient = jnp.concatenate([back_grad[1:], head_grads[tick][None]], axis=0)
    divisor = math.sqrt(TICKS * IMG_H * IMG_W)
    return (kernel_total / divisor, back_grad)
```

```python
import functools
import math

import jax
import jax.numpy as jnp
from jax import lax
from jax.experimental import pallas as pl
from jax.experimental.pallas import tpu as pltpu
from jax.sharding import PartitionSpec as P

MESH = pl.DeviceIdType.MESH
F32 = jnp.float32
BF16 = jnp.bfloat16
T, H, W, C = 4, 16, 32, 256
PX = H * W
HALF = PX // 2
GRID = PX + 2 * W
SECTIONS, TILES, RING = 32, 16, 8
ROWS = 9 * C // TILES
MESSAGES = 2 * (RING - 1)
TN = (((0,), (0,)), ((), ()))
NT = (((1,), (1,)), ((), ()))


def loop(count, step, start=0):
    def one(i, carry):
        step(i)
        return carry

    lax.fori_loop(start, count, one, 0)


def kernel(
    x_hbm, m_hbm, gin_hbm, head_hbm, w_hbm, sc_hbm, kg_ref, out_ref,
    xv, mv, wv, sv, gb, pg, bg, acc, xt, edge_i, edge, mh, sbuf, rbuf, zs, zr,
    ld_x, ld_m, ld_w, ld_s, ld_e,
    gm_send, gm_recv, gh_send, gh_recv, hh_send, mh_send, mh_recv,
    rs_send, rs_recv, z_send, z_recv,
):
    s = lax.axis_index("section")
    j = lax.axis_index("tile")
    z, y = j // RING, j % RING
    up_ok, down_ok = j > 0, j < TILES - 1
    sends, takes = s > 0, s < SECTIONS - 1
    top = s == SECTIONS - 1

    def ring(distance):
        return z * RING + (y + distance + RING) % RING

    partner = (j + RING) % TILES

    barrier = pltpu.get_barrier_semaphore()

    def greet(section, tile):
        pl.semaphore_signal(barrier, inc=1, device_id=(section, tile), device_id_type=MESH)

    greet(s, ring(1))
    greet(s, ring(-1))
    greet(s, partner)
    pl.when(up_ok)(lambda: greet(s, j - 1))
    pl.when(down_ok)(lambda: greet(s, j + 1))

    @pl.when(takes)
    def _():
        greet(s + 1, j)
        pl.when(up_ok)(lambda: greet(s + 1, j - 1))
        pl.when(down_ok)(lambda: greet(s + 1, j + 1))

    def rows_of(h):
        return pl.ds(h * HALF, HALF)

    def edge_load(side):
        return pltpu.make_async_copy(
            m_hbm.at[:, pl.ds(side * (PX - W), W), :], edge_i.at[side], ld_e.at[side]
        )

    def first_load(h):
        return pltpu.make_async_copy(
            gin_hbm.at[rows_of(h)], gb.at[0, pl.ds(W + h * HALF, HALF)], gm_recv.at[0, h]
        )

    def head_load(t, h):
        return pltpu.make_async_copy(
            head_hbm.at[t, rows_of(h)], gb.at[t + 1, pl.ds(W + h * HALF, HALF)], gm_recv.at[t + 1, h]
        )

    def mask_load(t):
        return pltpu.make_async_copy(m_hbm.at[t], mv.at[t], ld_m.at[t])

    def x_load(t):
        return pltpu.make_async_copy(x_hbm.at[t], xv.at[t], ld_x.at[t])

    w_load = pltpu.make_async_copy(w_hbm, wv, ld_w)
    s_load = pltpu.make_async_copy(sc_hbm, sv, ld_s)
    edge_load(0).start()
    edge_load(1).start()
    s_load.start()
    first_load(0).start()
    first_load(1).start()
    mask_load(0).start()
    w_load.start()
    x_load(0).start()
    x_load(T - 1).start()
    for t in range(1, T):
        mask_load(t).start()
    for t in range(1, T - 1):
        x_load(t).start()

    @pl.when(top)
    def _():
        for t in range(T - 1):
            head_load(t, 0).start()
            head_load(t, 1).start()

    def clear(i):
        acc[pl.ds(pl.multiple_of(i * C, C), C), :] = jnp.zeros((C, C), F32)

    loop(9, clear)
    edge_load(0).wait()
    edge_load(1).wait()
    edge[...] = edge_i[...].astype(BF16)

    greeted = 3 + up_ok.astype(jnp.int32) + down_ok.astype(jnp.int32)
    greeted = greeted + jnp.where(sends, greeted - 2, 0)
    pl.semaphore_wait(barrier, greeted)

    def to_tile(src, dst, send, recv, section, tile):
        return pltpu.make_async_remote_copy(
            src_ref=src, dst_ref=dst, send_sem=send, recv_sem=recv,
            device_id=(section, tile), device_id_type=MESH,
        )

    def halo(t, side):
        return gb.at[t, pl.ds(side * (PX + W), W)]

    def edge_rows(side):
        return pl.ds(side * (PX - W), W)

    def first_edge(side):
        return to_tile(
            gin_hbm.at[edge_rows(side)], halo(0, 1 - side),
            gh_send.at[0, side], gh_recv.at[0, 1 - side], s, j - 1 + 2 * side,
        )

    def mask_edge(side):
        return to_tile(
            edge.at[side], mh.at[1 - side], mh_send.at[side], mh_recv.at[1 - side], s, j - 1 + 2 * side
        )

    def head_edge(t, side):
        return to_tile(
            head_hbm.at[t, edge_rows(side)], halo(t + 1, 1 - side),
            hh_send.at[t, side], gh_recv.at[t + 1, 1 - side], s, j - 1 + 2 * side,
        )

    def back_edge(t, side):
        return to_tile(
            bg.at[t, edge_rows(side)], halo(t + 1, 1 - side),
            gh_send.at[t + 1, side], gh_recv.at[t + 1, 1 - side], s - 1, j - 1 + 2 * side,
        )

    def back_half(t, h):
        return to_tile(
            bg.at[t, rows_of(h)], gb.at[t + 1, pl.ds(W + h * HALF, HALF)],
            gm_send.at[t, h], gm_recv.at[t + 1, h], s - 1, j,
        )

    has_tile = (up_ok, down_ok)

    for side in range(2):

        @pl.when(has_tile[side])
        def _(side=side):
            first_edge(side).start()
            mask_edge(side).start()

            @pl.when(top)
            def _():
                for t in range(T - 1):
                    head_edge(t, side).start()

    s_load.wait()
    scales = sv[...]

    def column_shifts(t, at, value):
        count = value.shape[0]
        column = lax.broadcasted_iota(jnp.int32, (count, C), 0) % W
        dst = pl.ds(at, count)
        right = jnp.where(column == W - 1, 0.0, pltpu.roll(value, count - 1, 0))
        left = jnp.where(column == 0, 0.0, pltpu.roll(value, 1, 0))
        pg[3 * t, dst, :] = right.astype(BF16)
        pg[3 * t + 1, dst, :] = value.astype(BF16)
        pg[3 * t + 2, dst, :] = left.astype(BF16)

    def pre_grad(t):
        mask_load(t).wait()
        for h in range(2):
            pltpu.make_async_copy(
                gin_hbm.at[rows_of(h)], gb.at[t, pl.ds(W + h * HALF, HALF)], gm_recv.at[t, h]
            ).wait()

        def main(h):
            at = pl.multiple_of(h * HALF, HALF)
            grads = gb[t, pl.ds(W + at, HALF), :].astype(F32)
            value = jnp.where(mv[t, pl.ds(at, HALF), :] != 0, grads * scales, 0.0)
            column_shifts(t, W + at, value)

        loop(2, main)
        for side in range(2):
            at = side * (PX + W)

            @pl.when(has_tile[side])
            def _(side=side, at=at):
                pltpu.make_async_copy(
                    gin_hbm.at[edge_rows(side)], halo(t, side), gh_recv.at[t, side]
                ).wait()
                grads = gb[t, pl.ds(at, W), :].astype(F32)
                value = grads * mh[side, t].astype(F32) * scales
                column_shifts(t, at, value)

            @pl.when(jnp.logical_not(has_tile[side]))
            def _(at=at):
                for b in range(3):
                    pg[3 * t + b, pl.ds(at, W), :] = jnp.zeros((W, C), BF16)

    def conv(t, at, count):
        total = None
        for a in range(3):
            rows = pl.ds(pl.multiple_of((2 - a) * W + at, W), count)
            for b in range(3):
                term = lax.dot_general(
                    pg[3 * t + b, rows, :], wv[(3 * a + b) * C : (3 * a + b + 1) * C, :],
                    NT, preferred_element_type=F32,
                )
                total = term if total is None else total + term
        return total.astype(BF16)

    def kernel_term(t):
        def one(a):
            rows = pl.ds(pl.multiple_of((2 - a) * W, W), PX)
            for b in range(3):
                dst = pl.ds(pl.multiple_of((3 * a + b) * C, C), C)
                acc[dst, :] += lax.dot_general(
                    xv[t], pg[3 * t + b, rows, :], TN, preferred_element_type=F32
                )

        loop(3, one)

    for side in range(2):

        @pl.when(has_tile[side])
        def _(side=side):
            pltpu.make_async_copy(edge.at[side], mh.at[side], mh_recv.at[side]).wait()

    w_load.wait()

    def tick(t):
        pre_grad(t)
        for h in range(2):
            bg[t, rows_of(h), :] = conv(t, h * HALF, HALF)

            @pl.when(sends)
            def _(h=h):
                pl.when(has_tile[h])(lambda: back_edge(t, h).start())
                back_half(t, h).start()

        x_load(t).wait()
        kernel_term(t)

    loop(T - 1, tick)

    x_load(T - 1).wait()
    turned = xv[T - 1].T
    xt[0:C, :] = turned
    xt[C : 2 * C, :] = turned

    last = T - 1
    pre_grad(last)

    def block_row(i):
        k = i + 2
        away = RING // 2 - k // 4
        near = jnp.logical_or(k % 4 == 0, k % 4 == 3)
        owner_y = (y + jnp.where(i % 2 == 0, away, -away) + RING) % RING
        owner_z = jnp.where(near, z, 1 - z)
        return owner_z * RING + owner_y

    def block_of(i):
        return pl.ds(pl.multiple_of(block_row(i) * ROWS, 16), ROWS)

    def message(i):
        return to_tile(
            sbuf.at[i], rbuf.at[i], rs_send.at[i], rs_recv.at[i], s, ring(1 - 2 * (i % 2))
        )

    def first_messages(i):
        row0 = block_row(i) * ROWS
        tap = row0 // C
        at = pl.multiple_of(row0 - tap * C, 16)
        lhs = xt[pl.ds(at, ROWS), :]

        def term(tap):
            a, b = tap // 3, tap % 3
            rows = pl.ds(pl.multiple_of((2 - a) * W, W), PX)
            return jnp.dot(lhs, pg[3 * last + b, rows, :], preferred_element_type=F32)

        row = lax.broadcasted_iota(jnp.int32, (ROWS, C), 0) + at
        own = jnp.where(row < C, term(tap), term(jnp.minimum(tap + 1, 8)))
        sbuf[i] = (acc[block_of(i), :] + own).astype(BF16)
        message(i).start()

    def pass_on(i):
        message(i - 4).wait_recv()
        sbuf[i] = (acc[block_of(i), :] + rbuf[i - 4].astype(F32)).astype(BF16)
        message(i).start()

    loop(4, first_messages)
    kernel_term(last)
    loop(8, pass_on, 4)
    out_ref[...] = conv(last, 0, PX)
    loop(MESSAGES, pass_on, 8)

    m = MESSAGES
    message(m - 3).wait_recv()
    message(m - 2).wait_recv()
    total = acc[block_of(m + 1), :] + rbuf[m - 3].astype(F32) + rbuf[m - 2].astype(F32)
    zs[...] = total.astype(BF16)
    across = to_tile(zs, zr, z_send, z_recv, s, partner)
    across.start()
    message(m - 4).wait_recv()
    message(m - 1).wait_recv()
    total = acc[block_of(m), :] + rbuf[m - 4].astype(F32) + rbuf[m - 1].astype(F32)
    across.wait_recv()
    kg_ref[...] = (total + zr[...].astype(F32)) * (1.0 / math.sqrt(T * TILES * PX))

    across.wait_send()
    loop(MESSAGES, lambda i: message(i).wait_send())
    for side in range(2):

        @pl.when(has_tile[side])
        def _(side=side):
            first_edge(side).wait_send()
            mask_edge(side).wait_send()

            @pl.when(top)
            def _():
                for t in range(T - 1):
                    head_edge(t, side).wait_send()

            @pl.when(sends)
            def _():
                for t in range(T - 1):
                    back_edge(t, side).wait_send()

    @pl.when(sends)
    def _():
        for t in range(T - 1):
            back_half(t, 0).wait_send()
            back_half(t, 1).wait_send()


def per_device(saved_inputs, relu_mask, grads_in, head_grads, kernels, bn_scale):
    any_space = pl.BlockSpec(memory_space=pl.ANY)
    vmem = pl.BlockSpec(memory_space=pltpu.VMEM)
    dma = pltpu.SemaphoreType.DMA
    kernel_grads, outgoing = pl.pallas_call(
        kernel,
        out_shape=(
            jax.ShapeDtypeStruct((ROWS, C), F32),
            jax.ShapeDtypeStruct((PX, C), BF16),
        ),
        in_specs=[any_space] * 6,
        out_specs=(vmem, vmem),
        scratch_shapes=[
            pltpu.VMEM((T, PX, C), BF16),
            pltpu.VMEM((T, PX, C), jnp.int32),
            pltpu.VMEM((9 * C, C), BF16),
            pltpu.VMEM((1, C), F32),
            pltpu.VMEM((T, GRID, C), BF16),
            pltpu.VMEM((3 * T, GRID, C), BF16),
            pltpu.VMEM((T - 1, PX, C), BF16),
            pltpu.VMEM((9 * C, C), F32),
            pltpu.VMEM((2 * C, PX), BF16),
            pltpu.VMEM((2, T, W, C), jnp.int32),
            pltpu.VMEM((2, T, W, C), BF16),
            pltpu.VMEM((2, T, W, C), BF16),
            pltpu.VMEM((MESSAGES, ROWS, C), BF16),
            pltpu.VMEM((MESSAGES, ROWS, C), BF16),
            pltpu.VMEM((ROWS, C), BF16),
            pltpu.VMEM((ROWS, C), BF16),
            dma((T,)),
            dma((T,)),
            dma,
            dma,
            dma((2,)),
            dma((T - 1, 2)),
            dma((T, 2)),
            dma((T, 2)),
            dma((T, 2)),
            dma((T - 1, 2)),
            dma((2,)),
            dma((2,)),
            dma((MESSAGES,)),
            dma((MESSAGES,)),
            dma,
            dma,
        ],
        compiler_params=pltpu.CompilerParams(
            collective_id=0, has_side_effects=True, vmem_limit_bytes=48 * 2**20
        ),
        cost_estimate=pl.CostEstimate(
            flops=4 * T * PX * 9 * C * C, bytes_accessed=6 * 2**20, transcendentals=0
        ),
    )(
        saved_inputs.reshape(T, PX, C),
        relu_mask.reshape(T, PX, C),
        grads_in.reshape(PX, C),
        head_grads.reshape(T - 1, PX, C),
        kernels.reshape(9 * C, C),
        bn_scale,
    )
    return kernel_grads[None], outgoing.reshape(1, H, W, C)


def solution(mesh):
    return jax.shard_map(
        per_device,
        mesh=mesh,
        in_specs=(
            P("section", None, "tile", None, None),
            P("section", None, "tile", None, None),
            P("section", "tile", None, None),
            P(None, "tile", None, None),
            P("section", None, None, None, None),
            P("section", None),
        ),
        out_specs=(P("section", "tile", None), P("section", "tile", None, None)),
        check_vma=False,
    )
```

```python
import functools
import math

import jax
import jax.numpy as jnp
from jax import lax
from jax.experimental import pallas as pl
from jax.experimental.pallas import tpu as pltpu
from jax.sharding import PartitionSpec as P

MESH = pl.DeviceIdType.MESH
F32 = jnp.float32
BF16 = jnp.bfloat16
T, H, W, C = 4, 16, 32, 256
PX = H * W
LEAD = 2
GRID = PX + 2 * LEAD * W
SECTIONS, TILES, RING = 32, 16, 8
ROWS = 9 * C // TILES
PIECES = ((0, 80), (80, 64))
PLAN = {
    "F4+": (1, 4, 1, None), "F3+": (1, 3, 1, "F4+"), "F2+": (1, 2, 1, "F3+"), "F1+": (1, 1, 1, "F2+"),
    "F3-": (1, 3, -1, None), "F2-": (1, 2, -1, "F3-"), "F1-": (1, 1, -1, "F2-"), "F0": (1, 0, 0, None),
    "N3+": (0, 3, 1, None), "N2+": (0, 2, 1, "N3+"), "N1+": (0, 1, 1, "N2+"),
    "N4-": (0, 4, -1, None), "N3-": (0, 3, -1, "N4-"), "N2-": (0, 2, -1, "N3-"), "N1-": (0, 1, -1, "N2-"),
}
ORDER = (
    "F4+", "F3-", "N4-", "N3+", "F0", "F3+", "F2-", "N3-", "N2+", "F2+", "F1-", "N2-", "F1+", "N1+", "N1-",
)
FIRST = 4
TN = (((0,), (0,)), ((), ()))
NT = (((1,), (1,)), ((), ()))


def loop(count, step, start=0):
    def one(i, carry):
        step(i)
        return carry

    lax.fori_loop(start, count, one, 0)


def kernel(
    x_hbm, m_hbm, gin_hbm, head_hbm, w_hbm, sc_hbm, kg_ref, out_ref,
    xv, mv, wv, sv, gb, pg, bg, acc, xt, edge_i, edge, mh, sbuf, rbuf,
    ld_x, ld_m, ld_w, ld_s, ld_e,
    gm_send, gm_recv, ge_send, ge_recv, gd_send, gd_recv, hh_send,
    p0_send, p0_recv, mh_send, mh_recv, rs_send, rs_recv,
):
    s = lax.axis_index("section")
    j = lax.axis_index("tile")
    z, y = j // RING, j % RING
    has_tile = (j > 0, j < TILES - 1)
    sends, takes = s > 0, s < SECTIONS - 1
    top = s == SECTIONS - 1
    last = T - 1

    def ring(distance, other=0):
        row = (z + other) % 2
        return row * RING + (y + distance + RING) % RING

    def beside(side):
        return j - 1 + 2 * side

    barrier = pltpu.get_barrier_semaphore()

    def greet(section, tile):
        pl.semaphore_signal(barrier, inc=1, device_id=(section, tile), device_id_type=MESH)

    for distance, other in ((1, 0), (-1, 0), (0, 1), (1, 1), (-1, 1)):
        greet(s, ring(distance, other))
    for side in range(2):
        pl.when(has_tile[side])(lambda side=side: greet(s, beside(side)))

    @pl.when(takes)
    def _():
        greet(s + 1, j)
        for side in range(2):
            pl.when(has_tile[side])(lambda side=side: greet(s + 1, beside(side)))

    def rows(i, count=1, lead=LEAD):
        return pl.ds((i + lead) * W, count * W)

    def local(src, dst, sem):
        return pltpu.make_async_copy(src, dst, sem)

    def to_tile(src, dst, send, recv, section, tile):
        return pltpu.make_async_remote_copy(
            src_ref=src, dst_ref=dst, send_sem=send, recv_sem=recv,
            device_id=(section, tile), device_id_type=MESH,
        )

    def edge_load(side):
        return local(
            m_hbm.at[pl.ds(1, T - 1), rows(side * (H - 2), 2, 0), :], edge_i.at[side], ld_e.at[side]
        )

    def first_load(h):
        return local(
            gin_hbm.at[rows(h * (H // 2), H // 2, 0)], gb.at[0, rows(h * (H // 2), H // 2)], gm_recv.at[0, h]
        )

    def mask_load(t):
        return local(m_hbm.at[t], mv.at[t], ld_m.at[t])

    def x_load(t):
        return local(x_hbm.at[t], xv.at[t], ld_x.at[t])

    w_load = local(w_hbm, wv, ld_w)
    s_load = local(sc_hbm, sv, ld_s)
    s_load.start()
    first_load(0).start()
    first_load(1).start()
    mask_load(0).start()
    edge_load(0).start()
    edge_load(1).start()
    w_load.start()
    x_load(0).start()
    for t in range(1, T):
        mask_load(t).start()
        x_load(t).start()

    inner = {0: ((1, 7), (8, 7)), 1: ((2, 5), (7, 7)), 2: ((1, 7), (8, 7))}
    ends = {0: (-1, H - 1), 1: (0, H - 2), 2: (-1, H - 1)}

    def pass_inner(t, h):
        first, count = inner[t][h]
        return to_tile(
            bg.at[t, rows(first, count, 1)], gb.at[t + 1, rows(first, count)],
            gm_send.at[t, h], gm_recv.at[t + 1, h], s - 1, j,
        )

    def pass_end(t, side):
        return to_tile(
            bg.at[t, rows(ends[t][side], 2, 1)], gb.at[t + 1, rows(ends[t][side], 2)],
            ge_send.at[t, side], ge_recv.at[t + 1, side], s - 1, j,
        )

    def far(t, side):
        return gb.at[t, rows(H - (H + 2) * side, 2)]

    def pass_aside(side):
        return to_tile(
            bg.at[1, rows(ends[1][side], 2, 1)], far(2, side),
            gd_send.at[side], gd_recv.at[1 - side], s - 1, beside(side),
        )

    def first_aside(side):
        return to_tile(
            pg.at[1, rows(side * (H - 2), 2)], far(0, side),
            p0_send.at[side], p0_recv.at[1 - side], s, beside(side),
        )

    def mask_aside(side):
        return to_tile(
            edge.at[side], mh.at[1 - side], mh_send.at[side], mh_recv.at[1 - side], s, beside(side)
        )

    def head_local(t, first, count, sem):
        return local(head_hbm.at[t, rows(first, count, 0)], gb.at[t + 1, rows(first, count)], sem)

    def head_aside(t, side):
        if t == 1:
            src, dst, recv = rows(side * (H - 2), 2, 0), far(2, side), gd_recv.at[1 - side]
        else:
            src, dst, recv = rows(side * (H - 1), 1, 0), gb.at[t + 1, rows(H - (H + 1) * side)], ge_recv.at[t + 1, 1 - side]
        return to_tile(head_hbm.at[t, src], dst, hh_send.at[t, side], recv, s, beside(side))

    @pl.when(top)
    def _():
        for t in range(T - 1):
            for h in range(2):
                head_local(t, *inner[t][h], gm_recv.at[t + 1, h]).start()
            for side in range(2):
                sem = ge_recv.at[t + 1, side]
                if t == 1:
                    head_local(t, ends[t][side], 2, sem).start()
                else:
                    head_local(t, side * (H - 1), 1, sem).start()

                    @pl.when(jnp.logical_not(has_tile[side]))
                    def _(t=t, side=side, sem=sem):
                        local(
                            head_hbm.at[t, rows(side * (H - 1), 1, 0)],
                            gb.at[t + 1, rows(side * (H + 1) - 1)], sem,
                        ).start()

    def put(t, row, value):
        count = value.shape[0]
        column = lax.broadcasted_iota(jnp.int32, (count, C), 0) % W
        dst = pl.ds((row + LEAD) * W, count)
        right = jnp.where(column == W - 1, 0.0, pltpu.roll(value, count - 1, 0))
        left = jnp.where(column == 0, 0.0, pltpu.roll(value, 1, 0))
        pg[3 * t, dst, :] = right.astype(BF16)
        pg[3 * t + 1, dst, :] = value.astype(BF16)
        pg[3 * t + 2, dst, :] = left.astype(BF16)

    s_load.wait()
    scales = sv[...]

    def own_rows(t, first, count):
        grads = gb[t, rows(first, count), :].astype(F32)
        put(t, first, jnp.where(mv[t, rows(first, count, 0), :] != 0, grads * scales, 0.0))

    depth = (2, 1, 2, 1)
    mask_at = (None, 0, 1, 3)

    def beyond(t, side):
        count = depth[t]
        first = H if side else -count

        @pl.when(has_tile[side])
        def _():
            grads = gb[t, rows(first, count), :].astype(F32)
            if t:
                grads = grads * mh[side, rows(mask_at[t], count, 0), :].astype(F32) * scales
            put(t, first, grads)

        @pl.when(jnp.logical_not(has_tile[side]))
        def _():
            for b in range(3):
                pg[3 * t + b, rows(first, count), :] = jnp.zeros((count * W, C), BF16)

    def conv(t, starts, count):
        total = None
        for a in range(3):
            for b in range(3):
                parts = [pg[3 * t + b, rows(i + 1 - a, count), :] for i in starts]
                term = lax.dot_general(
                    parts[0] if len(parts) == 1 else jnp.concatenate(parts, axis=0),
                    wv[(3 * a + b) * C : (3 * a + b + 1) * C, :],
                    NT, preferred_element_type=F32,
                )
                total = term if total is None else total + term
        return total.astype(BF16)

    def inner_part(t, h):
        first, count = inner[t][h]
        bg[t, rows(first, count, 1), :] = conv(t, [first], count)
        pl.when(sends)(lambda: pass_inner(t, h).start())

    def end_parts(t):
        both = conv(t, ends[t], 2)
        for side in range(2):
            bg[t, rows(ends[t][side], 2, 1), :] = both[side * 2 * W : (side + 1) * 2 * W]

        @pl.when(sends)
        def _():
            for side in range(2):
                if t == 1:
                    pl.when(has_tile[side])(lambda side=side: pass_aside(side).start())
            for side in range(2):
                pass_end(t, side).start()

    def kernel_term(t):
        def one(a):
            taps = pl.ds(pl.multiple_of((LEAD + 1 - a) * W, W), PX)
            for b in range(3):
                dst = pl.ds(pl.multiple_of((3 * a + b) * C, C), C)
                acc[dst, :] += lax.dot_general(
                    xv[t], pg[3 * t + b, taps, :], TN, preferred_element_type=F32
                )

        loop(3, one)

    def got_inner(t, h):
        first, count = inner[t - 1][h]
        local(head_hbm.at[0, rows(first, count, 0)], gb.at[t, rows(first, count)], gm_recv.at[t, h]).wait()

    def got_end(t, side):
        local(head_hbm.at[0, rows(0, 2, 0)], gb.at[t, rows(ends[t - 1][side], 2)], ge_recv.at[t, side]).wait()

    first_load(0).wait()
    first_load(1).wait()
    mask_load(0).wait()
    own_rows(0, 0, 8)
    own_rows(0, 8, 8)
    for side in range(2):
        edge_load(side).wait()
        pick = pl.ds(side * W, W)
        edge[side, 0:W, :] = edge_i[side, 0, pick, :].astype(BF16)
        edge[side, W : 3 * W, :] = edge_i[side, 1, :, :].astype(BF16)
        edge[side, 3 * W : 4 * W, :] = edge_i[side, 2, pick, :].astype(BF16)

    beside_count = has_tile[0].astype(jnp.int32) + has_tile[1].astype(jnp.int32)
    pl.semaphore_wait(barrier, 5 + beside_count + jnp.where(sends, beside_count + 1, 0))

    for side in range(2):
        pl.when(has_tile[side])(lambda side=side: first_aside(side).start())
    for side in range(2):

        @pl.when(has_tile[side])
        def _(side=side):
            mask_aside(side).start()

            @pl.when(top)
            def _():
                for t in range(T - 1):
                    head_aside(t, side).start()

    w_load.wait()
    inner_part(0, 0)
    inner_part(0, 1)

    def clear(i):
        acc[pl.ds(pl.multiple_of(i * C, C), C), :] = jnp.zeros((C, C), F32)

    loop(9, clear)
    for side in range(2):
        pl.when(has_tile[side])(
            lambda side=side: local(gin_hbm.at[rows(0, 2, 0)], far(0, 1 - side), p0_recv.at[side]).wait()
        )
        beyond(0, side)
    end_parts(0)
    x_load(0).wait()
    kernel_term(0)

    mask_load(1).wait()
    got_inner(1, 0)
    own_rows(1, 1, 7)
    inner_part(1, 0)
    got_inner(1, 1)
    own_rows(1, 8, 7)
    inner_part(1, 1)
    for side in range(2):
        pl.when(has_tile[side])(
            lambda side=side: local(edge.at[side], mh.at[side], mh_recv.at[side]).wait()
        )
        got_end(1, side)
        own_rows(1, side * (H - 1), 1)
        beyond(1, side)
    end_parts(1)
    x_load(1).wait()
    kernel_term(1)

    mask_load(2).wait()
    got_inner(2, 0)
    own_rows(2, 2, 5)
    got_inner(2, 1)
    own_rows(2, 7, 7)
    for side in range(2):
        got_end(2, side)
        own_rows(2, side * (H - 2), 2)
    inner_part(2, 0)
    inner_part(2, 1)
    for side in range(2):
        pl.when(has_tile[side])(
            lambda side=side: local(gin_hbm.at[rows(0, 2, 0)], far(2, 1 - side), gd_recv.at[side]).wait()
        )
        beyond(2, side)
    end_parts(2)
    x_load(2).wait()
    kernel_term(2)

    x_load(last).wait()
    turned = xv[last].T
    xt[0:C, :] = turned
    xt[C : 2 * C, :] = turned
    mask_load(last).wait()
    got_inner(last, 0)
    own_rows(last, 1, 7)
    got_inner(last, 1)
    own_rows(last, 8, 7)
    for side in range(2):
        got_end(last, side)
        own_rows(last, side * (H - 1), 1)
        beyond(last, side)

    def block_row(name):
        kind, away, way, _ = PLAN[name]
        return ring(way * away, kind) * ROWS

    def piece(name, part, whole=False):
        start, count = (0, ROWS) if whole else PIECES[part]
        return pl.ds(pl.multiple_of(block_row(name) + start, 16), count)

    def message(name, part):
        kind, away, way, _ = PLAN[name]
        i = ORDER.index(name)
        at = pl.ds(*PIECES[part])
        crosses = kind == 1 and away <= 1
        return to_tile(
            sbuf.at[i, at], rbuf.at[i, at], rs_send.at[i, part], rs_recv.at[i, part],
            s, ring(way, 1 if crosses else 0),
        )

    def first_message(name):
        row0 = block_row(name)
        tap = row0 // C
        at = pl.multiple_of(row0 - tap * C, 16)
        lhs = xt[pl.ds(at, ROWS), :]

        def term(tap):
            a, b = tap // 3, tap % 3
            taps = pl.ds(pl.multiple_of((LEAD + 1 - a) * W, W), PX)
            return jnp.dot(lhs, pg[3 * last + b, taps, :], preferred_element_type=F32)

        row = lax.broadcasted_iota(jnp.int32, (ROWS, C), 0) + at
        own = jnp.where(row < C, term(tap), term(jnp.minimum(tap + 1, 8)))
        sbuf[ORDER.index(name)] = (acc[piece(name, 0, True), :] + own).astype(BF16)
        for part in range(2):
            message(name, part).start()

    def later_message(name, part):
        total = acc[piece(name, part), :]
        before = PLAN[name][3]
        at = pl.ds(*PIECES[part])
        if before:
            message(before, part).wait_recv()
            total = total + rbuf[ORDER.index(before), at, :].astype(F32)
        sbuf[ORDER.index(name), at, :] = total.astype(BF16)
        message(name, part).start()

    for name in ORDER[:FIRST]:
        first_message(name)
    kernel_term(last)
    for name in ORDER[FIRST:]:
        for part in range(2):
            later_message(name, part)
        if name == "F1-":
            out_ref[...] = conv(last, [0], H)

    for part in range(2):
        start, count = PIECES[part]
        at = pl.ds(start, count)
        total = acc[pl.ds(pl.multiple_of(j * ROWS + start, 16), count), :]
        for name in ("F0", "F1-", "N1+", "F1+", "N1-"):
            message(name, part).wait_recv()
            total = total + rbuf[ORDER.index(name), at, :].astype(F32)
        kg_ref[at, :] = total * (1.0 / math.sqrt(T * TILES * PX))

    for name in ORDER:
        for part in range(2):
            message(name, part).wait_send()
    for side in range(2):

        @pl.when(has_tile[side])
        def _(side=side):
            first_aside(side).wait_send()
            mask_aside(side).wait_send()
            pl.when(sends)(lambda: pass_aside(side).wait_send())

            @pl.when(top)
            def _():
                for t in range(T - 1):
                    head_aside(t, side).wait_send()

    @pl.when(sends)
    def _():
        for t in range(T - 1):
            for k in range(2):
                pass_inner(t, k).wait_send()
                pass_end(t, k).wait_send()


def per_device(saved_inputs, relu_mask, grads_in, head_grads, kernels, bn_scale):
    any_space = pl.BlockSpec(memory_space=pl.ANY)
    vmem = pl.BlockSpec(memory_space=pltpu.VMEM)
    dma = pltpu.SemaphoreType.DMA
    kernel_grads, outgoing = pl.pallas_call(
        kernel,
        out_shape=(
            pltpu.VMEM((ROWS, C), F32),
            pltpu.VMEM((PX, C), BF16),
        ),
        in_specs=[any_space] * 6,
        out_specs=(vmem, vmem),
        scratch_shapes=[
            pltpu.VMEM((T, PX, C), BF16),
            pltpu.VMEM((T, PX, C), jnp.int32),
            pltpu.VMEM((9 * C, C), BF16),
            pltpu.VMEM((1, C), F32),
            pltpu.VMEM((T, GRID, C), BF16),
            pltpu.VMEM((3 * T, GRID, C), BF16),
            pltpu.VMEM((T - 1, PX + 2 * W, C), BF16),
            pltpu.VMEM((9 * C, C), F32),
            pltpu.VMEM((2 * C, PX), BF16),
            pltpu.VMEM((2, T - 1, 2 * W, C), jnp.int32),
            pltpu.VMEM((2, 4 * W, C), BF16),
            pltpu.VMEM((2, 4 * W, C), BF16),
            pltpu.VMEM((len(ORDER), ROWS, C), BF16),
            pltpu.VMEM((len(ORDER), ROWS, C), BF16),
            dma((T,)),
            dma((T,)),
            dma,
            dma,
            dma((2,)),
            dma((T - 1, 2)),
            dma((T, 2)),
            dma((T - 1, 2)),
            dma((T, 2)),
            dma((2,)),
            dma((2,)),
            dma((T - 1, 2)),
            dma((2,)),
            dma((2,)),
            dma((2,)),
            dma((2,)),
            dma((len(ORDER), 2)),
            dma((len(ORDER), 2)),
        ],
        compiler_params=pltpu.CompilerParams(
            collective_id=0, has_side_effects=True, vmem_limit_bytes=62 * 2**20
        ),
        cost_estimate=pl.CostEstimate(
            flops=4 * T * PX * 9 * C * C, bytes_accessed=6 * 2**20, transcendentals=0
        ),
    )(
        saved_inputs.reshape(T, PX, C),
        relu_mask.reshape(T, PX, C),
        grads_in.reshape(PX, C),
        head_grads.reshape(T - 1, PX, C),
        kernels.reshape(9 * C, C),
        bn_scale,
    )
    return kernel_grads[None], outgoing.reshape(1, H, W, C)


def solution(mesh):
    return jax.shard_map(
        per_device,
        mesh=mesh,
        in_specs=(
            P("section", None, "tile", None, None),
            P("section", None, "tile", None, None),
            P("section", "tile", None, None),
            P(None, "tile", None, None),
            P("section", None, None, None, None),
            P("section", None),
        ),
        out_specs=(P("section", "tile", None), P("section", "tile", None, None)),
        check_vma=False,
    )
```

```python
import functools
import math

import jax
import jax.numpy as jnp
from jax import lax
from jax.experimental import pallas as pl
from jax.experimental.pallas import tpu as pltpu
from jax.sharding import PartitionSpec as P

MESH = pl.DeviceIdType.MESH
F32 = jnp.float32
BF16 = jnp.bfloat16
T, H, W, C = 4, 16, 32, 256
PX = H * W
LEAD = 4
GRID = PX + 2 * LEAD * W
SECTIONS, TILES, RING = 32, 16, 8
ROWS = 9 * C // TILES
PIECES = ((0, 80), (80, 64))
PLAN = {
    "F4+": (1, 4, 1, None), "F3+": (1, 3, 1, "F4+"), "F2+": (1, 2, 1, "F3+"), "F1+": (1, 1, 1, "F2+"),
    "F3-": (1, 3, -1, None), "F2-": (1, 2, -1, "F3-"), "F1-": (1, 1, -1, "F2-"), "F0": (1, 0, 0, None),
    "N3+": (0, 3, 1, None), "N2+": (0, 2, 1, "N3+"), "N1+": (0, 1, 1, "N2+"),
    "N4-": (0, 4, -1, None), "N3-": (0, 3, -1, "N4-"), "N2-": (0, 2, -1, "N3-"), "N1-": (0, 1, -1, "N2-"),
}
ORDER = (
    "F4+", "F3-", "N4-", "N3+", "F0", "F3+", "F2-", "N3-", "N2+", "F2+", "F1-", "N2-", "F1+", "N1+", "N1-",
)
FIRST = 4
TN = (((0,), (0,)), ((), ()))
NT = (((1,), (1,)), ((), ()))


def loop(count, step, start=0):
    def one(i, carry):
        step(i)
        return carry

    lax.fori_loop(start, count, one, 0)


def kernel(
    x_hbm, m_hbm, gin_hbm, head_hbm, w_hbm, sc_hbm, kg_ref, out_ref,
    xv, mv, wv, sv, gb, pg, bg, acc, xt, edge, mh, sbuf, rbuf,
    ld_x, ld_m, ld_w, ld_s,
    gm_send, gm_recv, ge_send, ge_recv, gd_send, gd_recv, gx_send, gx_recv, hh_send, hx_send,
    p0_send, p0_recv, mh_send, mh_recv, rs_send, rs_recv,
):
    s = lax.axis_index("section")
    j = lax.axis_index("tile")
    z, y = j // RING, j % RING
    has_tile = (j > 0, j < TILES - 1)
    seam = (j == RING, j == RING - 1)
    near = tuple(jnp.logical_and(a, jnp.logical_not(b)) for a, b in zip(has_tile, seam))
    sends, takes = s > 0, s < SECTIONS - 1
    top = s == SECTIONS - 1
    last = T - 1

    def ring(distance, other=0):
        row = (z + other) % 2
        return row * RING + (y + distance + RING) % RING

    def beside(side):
        return j - 1 + 2 * side

    barrier = pltpu.get_barrier_semaphore()

    def greet(section, tile):
        pl.semaphore_signal(barrier, inc=1, device_id=(section, tile), device_id_type=MESH)

    for side in range(2):
        pl.when(has_tile[side])(lambda side=side: greet(s, beside(side)))
    for distance, other in ((1, 0), (-1, 0), (0, 1), (1, 1), (-1, 1)):
        greet(s, ring(distance, other))

    @pl.when(takes)
    def _():
        greet(s + 1, j)
        for side in range(2):
            pl.when(near[side])(lambda side=side: greet(s + 1, beside(side)))

    def rows(i, count=1, lead=LEAD):
        return pl.ds((i + lead) * W, count * W)

    def local(src, dst, sem):
        return pltpu.make_async_copy(src, dst, sem)

    def to_tile(src, dst, send, recv, section, tile):
        return pltpu.make_async_remote_copy(
            src_ref=src, dst_ref=dst, send_sem=send, recv_sem=recv,
            device_id=(section, tile), device_id_type=MESH,
        )

    def first_load(h):
        return local(
            gin_hbm.at[rows(h * (H // 2), H // 2, 0)], gb.at[0, rows(h * (H // 2), H // 2)], gm_recv.at[0, h]
        )

    def mask_load(t):
        return local(m_hbm.at[t], mv.at[t], ld_m.at[t])

    def x_load(t):
        return local(x_hbm.at[t], xv.at[t], ld_x.at[t])

    w_load = local(w_hbm, wv, ld_w)
    s_load = local(sc_hbm, sv, ld_s)
    s_load.start()
    first_load(0).start()
    first_load(1).start()
    for t in range(T):
        mask_load(t).start()
    w_load.start()
    for t in range(T):
        x_load(t).start()

    inner = {0: ((1, 7), (8, 7)), 1: ((2, 5), (7, 7)), 2: ((1, 7), (8, 7))}
    ends = {0: (-1, H - 1), 1: (0, H - 2), 2: (-1, H - 1)}

    def pass_inner(t, h):
        first, count = inner[t][h]
        return to_tile(
            bg.at[t, rows(first, count, 3)], gb.at[t + 1, rows(first, count)],
            gm_send.at[t, h], gm_recv.at[t + 1, h], s - 1, j,
        )

    def pass_end(t, side):
        return to_tile(
            bg.at[t, rows(ends[t][side], 2, 3)], gb.at[t + 1, rows(ends[t][side], 2)],
            ge_send.at[t, side], ge_recv.at[t + 1, side], s - 1, j,
        )

    extra = ((-3, H + 1), (-2, H))

    def pass_extra(t, side):
        send, recv = ((gx_send, gx_recv), (gd_send, gd_recv))[t]
        return to_tile(
            bg.at[t, rows(extra[t][side], 2, 3)], gb.at[t + 1, rows(extra[t][side], 2)],
            send.at[side], recv.at[side], s - 1, j,
        )

    def far(t, side, count=2):
        return gb.at[t, rows(H - (H + count) * side, count)]

    def pass_aside(side):
        return to_tile(
            bg.at[1, rows(ends[1][side], 2, 3)], far(2, side),
            gd_send.at[side], gd_recv.at[1 - side], s - 1, beside(side),
        )

    def first_aside(side, count):
        return to_tile(
            pg.at[1, rows(side * (H - count), count)], far(0, side, count),
            p0_send.at[side], p0_recv.at[1 - side], s, beside(side),
        )

    def mask_aside(side):
        return to_tile(
            edge.at[side], mh.at[1 - side], mh_send.at[side], mh_recv.at[1 - side], s, beside(side)
        )

    def head_local(t, first, count, sem):
        return local(head_hbm.at[t, rows(first, count, 0)], gb.at[t + 1, rows(first, count)], sem)

    def head_aside(t, side):
        if t == 1:
            src, dst, recv = rows(side * (H - 2), 2, 0), far(2, side), gd_recv.at[1 - side]
        else:
            src, dst, recv = rows(side * (H - 1), 1, 0), gb.at[t + 1, rows(H - (H + 1) * side)], ge_recv.at[t + 1, 1 - side]
        return to_tile(head_hbm.at[t, src], dst, hh_send.at[t, side], recv, s, beside(side))

    def head_extra(side):
        return to_tile(
            head_hbm.at[0, rows(1 + side * (H - 4), 2, 0)], gb.at[1, rows(H + 1 - (H + 4) * side, 2)],
            hx_send.at[side], gx_recv.at[1 - side], s, beside(side),
        )

    @pl.when(top)
    def _():
        for t in range(T - 1):
            for h in range(2):
                head_local(t, *inner[t][h], gm_recv.at[t + 1, h]).start()
            for side in range(2):
                sem = ge_recv.at[t + 1, side]
                if t == 1:
                    head_local(t, ends[t][side], 2, sem).start()
                else:
                    head_local(t, side * (H - 1), 1, sem).start()

                    @pl.when(jnp.logical_not(has_tile[side]))
                    def _(t=t, side=side, sem=sem):
                        local(
                            head_hbm.at[t, rows(side * (H - 1), 1, 0)],
                            gb.at[t + 1, rows(side * (H + 1) - 1)], sem,
                        ).start()

    def put(t, row, value):
        count = value.shape[0]
        column = lax.broadcasted_iota(jnp.int32, (count, C), 0) % W
        dst = pl.ds((row + LEAD) * W, count)
        right = jnp.where(column == W - 1, 0.0, pltpu.roll(value, count - 1, 0))
        left = jnp.where(column == 0, 0.0, pltpu.roll(value, 1, 0))
        pg[3 * t, dst, :] = right.astype(BF16)
        pg[3 * t + 1, dst, :] = value.astype(BF16)
        pg[3 * t + 2, dst, :] = left.astype(BF16)

    s_load.wait()
    scales = sv[...]

    def own_rows(t, first, count):
        grads = gb[t, rows(first, count), :].astype(F32)
        put(t, first, jnp.where(mv[t, rows(first, count, 0), :] != 0, grads * scales, 0.0))

    depth, seam_depth = (2, 1, 2, 1), (4, 3, 2, 1)
    mask_at = (None, 0, 3, 5)

    def beyond(t, side):
        def fill(count):
            first = H if side else -count
            grads = gb[t, rows(first, count), :].astype(F32)
            if t:
                at = mask_at[t] + (0 if side else seam_depth[t] - count)
                grads = grads * mh[side, rows(at, count, 0), :].astype(F32) * scales
            put(t, first, grads)

        if t < 2:
            pl.when(near[side])(lambda: fill(depth[t]))
            pl.when(seam[side])(lambda: fill(seam_depth[t]))
        else:
            pl.when(has_tile[side])(lambda: fill(depth[t]))

        @pl.when(jnp.logical_not(has_tile[side]))
        def _():
            for b in range(3):
                pg[3 * t + b, rows(H if side else -depth[t], depth[t]), :] = jnp.zeros((depth[t] * W, C), BF16)

    def conv(t, starts, count):
        total = None
        for a in range(3):
            for b in range(3):
                parts = [pg[3 * t + b, rows(i + 1 - a, count), :] for i in starts]
                term = lax.dot_general(
                    parts[0] if len(parts) == 1 else jnp.concatenate(parts, axis=0),
                    wv[(3 * a + b) * C : (3 * a + b + 1) * C, :],
                    NT, preferred_element_type=F32,
                )
                total = term if total is None else total + term
        return total.astype(BF16)

    def inner_part(t, h):
        first, count = inner[t][h]
        bg[t, rows(first, count, 3), :] = conv(t, [first], count)
        pl.when(sends)(lambda: pass_inner(t, h).start())

    def end_parts(t):
        both = conv(t, ends[t], 2)
        for side in range(2):
            bg[t, rows(ends[t][side], 2, 3), :] = both[side * 2 * W : (side + 1) * 2 * W]

        @pl.when(sends)
        def _():
            for side in range(2):
                if t == 1:
                    pl.when(near[side])(lambda side=side: pass_aside(side).start())
            for side in range(2):
                pass_end(t, side).start()
            if t < 2:
                for side in range(2):

                    @pl.when(seam[side])
                    def _(side=side):
                        bg[t, rows(extra[t][side], 2, 3), :] = conv(t, [extra[t][side]], 2)
                        pass_extra(t, side).start()

    def kernel_term(t):
        def one(a):
            taps = pl.ds(pl.multiple_of((LEAD + 1 - a) * W, W), PX)
            for b in range(3):
                dst = pl.ds(pl.multiple_of((3 * a + b) * C, C), C)
                acc[dst, :] += lax.dot_general(
                    xv[t], pg[3 * t + b, taps, :], TN, preferred_element_type=F32
                )

        loop(3, one)

    def got_inner(t, h):
        first, count = inner[t - 1][h]
        local(head_hbm.at[0, rows(first, count, 0)], gb.at[t, rows(first, count)], gm_recv.at[t, h]).wait()

    def got_end(t, side):
        local(head_hbm.at[0, rows(0, 2, 0)], gb.at[t, rows(ends[t - 1][side], 2)], ge_recv.at[t, side]).wait()

    first_load(0).wait()
    first_load(1).wait()
    mask_load(0).wait()
    own_rows(0, 0, 8)
    own_rows(0, 8, 8)
    for t in range(1, T):
        mask_load(t).wait()
        count = seam_depth[t]
        for side in range(2):
            edge[side, rows(mask_at[t], count, 0), :] = mv[t, rows(side * (H - count), count, 0), :].astype(BF16)

    def flags(pair):
        return pair[0].astype(jnp.int32) + pair[1].astype(jnp.int32)

    pl.semaphore_wait(barrier, 5 + flags(has_tile) + jnp.where(sends, flags(near) + 1, 0))

    for side in range(2):
        pl.when(near[side])(lambda side=side: first_aside(side, 2).start())
        pl.when(seam[side])(lambda side=side: first_aside(side, 4).start())
    for side in range(2):

        @pl.when(has_tile[side])
        def _(side=side):
            mask_aside(side).start()

            @pl.when(top)
            def _():
                for t in range(T - 1):
                    head_aside(t, side).start()
                pl.when(seam[side])(lambda: head_extra(side).start())

    w_load.wait()
    inner_part(0, 0)
    inner_part(0, 1)

    def clear(i):
        acc[pl.ds(pl.multiple_of(i * C, C), C), :] = jnp.zeros((C, C), F32)

    loop(9, clear)

    def got_far(t, side, count, sem):
        local(gin_hbm.at[rows(0, count, 0)], far(t, 1 - side, count), sem.at[side]).wait()

    for side in range(2):
        pl.when(near[side])(lambda side=side: got_far(0, side, 2, p0_recv))
        pl.when(seam[side])(lambda side=side: got_far(0, side, 4, p0_recv))
        beyond(0, side)
    end_parts(0)

    got_inner(1, 0)
    own_rows(1, 1, 7)
    inner_part(1, 0)
    got_inner(1, 1)
    own_rows(1, 8, 7)
    inner_part(1, 1)
    x_load(0).wait()
    kernel_term(0)

    for side in range(2):
        pl.when(has_tile[side])(
            lambda side=side: local(edge.at[side], mh.at[side], mh_recv.at[side]).wait()
        )
        pl.when(seam[side])(
            lambda side=side: local(
                gin_hbm.at[rows(0, 2, 0)], gb.at[1, rows(extra[0][side], 2)], gx_recv.at[side]
            ).wait()
        )
        got_end(1, side)
        own_rows(1, side * (H - 1), 1)
        beyond(1, side)
    end_parts(1)
    x_load(1).wait()
    kernel_term(1)

    got_inner(2, 0)
    own_rows(2, 2, 5)
    got_inner(2, 1)
    own_rows(2, 7, 7)
    for side in range(2):
        got_end(2, side)
        own_rows(2, side * (H - 2), 2)
    inner_part(2, 0)
    inner_part(2, 1)
    for side in range(2):
        pl.when(has_tile[side])(lambda side=side: got_far(2, side, 2, gd_recv))
        beyond(2, side)
    end_parts(2)
    x_load(2).wait()
    kernel_term(2)

    x_load(last).wait()
    turned = xv[last].T
    xt[0:C, :] = turned
    xt[C : 2 * C, :] = turned
    got_inner(last, 0)
    own_rows(last, 1, 7)
    got_inner(last, 1)
    own_rows(last, 8, 7)
    for side in range(2):
        got_end(last, side)
        own_rows(last, side * (H - 1), 1)
        beyond(last, side)

    def block_row(name):
        kind, away, way, _ = PLAN[name]
        return ring(way * away, kind) * ROWS

    def piece(name, part, whole=False):
        start, count = (0, ROWS) if whole else PIECES[part]
        return pl.ds(pl.multiple_of(block_row(name) + start, 16), count)

    def message(name, part):
        kind, away, way, _ = PLAN[name]
        i = ORDER.index(name)
        at = pl.ds(*PIECES[part])
        crosses = kind == 1 and away <= 1
        return to_tile(
            sbuf.at[i, at], rbuf.at[i, at], rs_send.at[i, part], rs_recv.at[i, part],
            s, ring(way, 1 if crosses else 0),
        )

    def first_message(name):
        row0 = block_row(name)
        tap = row0 // C
        at = pl.multiple_of(row0 - tap * C, 16)
        lhs = xt[pl.ds(at, ROWS), :]

        def term(tap):
            a, b = tap // 3, tap % 3
            taps = pl.ds(pl.multiple_of((LEAD + 1 - a) * W, W), PX)
            return jnp.dot(lhs, pg[3 * last + b, taps, :], preferred_element_type=F32)

        row = lax.broadcasted_iota(jnp.int32, (ROWS, C), 0) + at
        own = jnp.where(row < C, term(tap), term(jnp.minimum(tap + 1, 8)))
        sbuf[ORDER.index(name)] = (acc[piece(name, 0, True), :] + own).astype(BF16)
        for part in range(2):
            message(name, part).start()

    def later_message(name, part):
        total = acc[piece(name, part), :]
        before = PLAN[name][3]
        at = pl.ds(*PIECES[part])
        if before:
            message(before, part).wait_recv()
            total = total + rbuf[ORDER.index(before), at, :].astype(F32)
        sbuf[ORDER.index(name), at, :] = total.astype(BF16)
        message(name, part).start()

    for name in ORDER[:FIRST]:
        first_message(name)
    kernel_term(last)
    for name in ORDER[FIRST:]:
        for part in range(2):
            later_message(name, part)
        if name == "F1-":
            out_ref[...] = conv(last, [0], H)

    for part in range(2):
        start, count = PIECES[part]
        at = pl.ds(start, count)
        total = acc[pl.ds(pl.multiple_of(j * ROWS + start, 16), count), :]
        for name in ("F0", "F1-", "N1+", "F1+", "N1-"):
            message(name, part).wait_recv()
            total = total + rbuf[ORDER.index(name), at, :].astype(F32)
        kg_ref[at, :] = total * (1.0 / math.sqrt(T * TILES * PX))

    for name in ORDER:
        for part in range(2):
            message(name, part).wait_send()
    for side in range(2):

        @pl.when(has_tile[side])
        def _(side=side):
            mask_aside(side).wait_send()

            @pl.when(top)
            def _():
                for t in range(T - 1):
                    head_aside(t, side).wait_send()
                pl.when(seam[side])(lambda: head_extra(side).wait_send())

        @pl.when(near[side])
        def _(side=side):
            first_aside(side, 2).wait_send()
            pl.when(sends)(lambda: pass_aside(side).wait_send())

        @pl.when(seam[side])
        def _(side=side):
            first_aside(side, 4).wait_send()

            @pl.when(sends)
            def _():
                pass_extra(0, side).wait_send()
                pass_extra(1, side).wait_send()

    @pl.when(sends)
    def _():
        for t in range(T - 1):
            for k in range(2):
                pass_inner(t, k).wait_send()
                pass_end(t, k).wait_send()


def per_device(saved_inputs, relu_mask, grads_in, head_grads, kernels, bn_scale):
    any_space = pl.BlockSpec(memory_space=pl.ANY)
    vmem = pl.BlockSpec(memory_space=pltpu.VMEM)
    dma = pltpu.SemaphoreType.DMA
    kernel_grads, outgoing = pl.pallas_call(
        kernel,
        out_shape=(
            pltpu.VMEM((ROWS, C), F32),
            pltpu.VMEM((PX, C), BF16),
        ),
        in_specs=[any_space] * 6,
        out_specs=(vmem, vmem),
        scratch_shapes=[
            pltpu.VMEM((T, PX, C), BF16),
            pltpu.VMEM((T, PX, C), jnp.int32),
            pltpu.VMEM((9 * C, C), BF16),
            pltpu.VMEM((1, C), F32),
            pltpu.VMEM((T, GRID, C), BF16),
            pltpu.VMEM((3 * T, GRID, C), BF16),
            pltpu.VMEM((T - 1, PX + 6 * W, C), BF16),
            pltpu.VMEM((9 * C, C), F32),
            pltpu.VMEM((2 * C, PX), BF16),
            pltpu.VMEM((2, 6 * W, C), BF16),
            pltpu.VMEM((2, 6 * W, C), BF16),
            pltpu.VMEM((len(ORDER), ROWS, C), BF16),
            pltpu.VMEM((len(ORDER), ROWS, C), BF16),
            dma((T,)),
            dma((T,)),
            dma,
            dma,
            dma((T - 1, 2)),
            dma((T, 2)),
            dma((T - 1, 2)),
            dma((T, 2)),
            dma((2,)),
            dma((2,)),
            dma((2,)),
            dma((2,)),
            dma((T - 1, 2)),
            dma((2,)),
            dma((2,)),
            dma((2,)),
            dma((2,)),
            dma((2,)),
            dma((len(ORDER), 2)),
            dma((len(ORDER), 2)),
        ],
        compiler_params=pltpu.CompilerParams(
            collective_id=0, has_side_effects=True, vmem_limit_bytes=62 * 2**20
        ),
        cost_estimate=pl.CostEstimate(
            flops=4 * T * PX * 9 * C * C, bytes_accessed=6 * 2**20, transcendentals=0
        ),
    )(
        saved_inputs.reshape(T, PX, C),
        relu_mask.reshape(T, PX, C),
        grads_in.reshape(PX, C),
        head_grads.reshape(T - 1, PX, C),
        kernels.reshape(9 * C, C),
        bn_scale,
    )
    return kernel_grads[None], outgoing.reshape(1, H, W, C)


def solution(mesh):
    return jax.shard_map(
        per_device,
        mesh=mesh,
        in_specs=(
            P("section", None, "tile", None, None),
            P("section", None, "tile", None, None),
            P("section", "tile", None, None),
            P(None, "tile", None, None),
            P("section", None, None, None, None),
            P("section", None),
        ),
        out_specs=(P("section", "tile", None), P("section", "tile", None, None)),
        check_vma=False,
    )
```

```python
import functools
import math

import jax
import jax.numpy as jnp
from jax import lax
from jax.experimental import pallas as pl
from jax.experimental.pallas import tpu as pltpu
from jax.sharding import PartitionSpec as P

MESH = pl.DeviceIdType.MESH
F32 = jnp.float32
BF16 = jnp.bfloat16
T, H, W, C = 4, 16, 32, 256
PX = H * W
LEAD = 2
GRID = PX + 2 * LEAD * W
SECTIONS, TILES, RING = 32, 16, 8
ROWS = 9 * C // TILES
PIECES = ((0, 80), (80, 64))
PLAN = {
    "F4+": (1, 4, 1, None), "F3+": (1, 3, 1, "F4+"), "F2+": (1, 2, 1, "F3+"), "F1+": (1, 1, 1, "F2+"),
    "F3-": (1, 3, -1, None), "F2-": (1, 2, -1, "F3-"), "F1-": (1, 1, -1, "F2-"), "F0": (1, 0, 0, None),
    "N3+": (0, 3, 1, None), "N2+": (0, 2, 1, "N3+"), "N1+": (0, 1, 1, "N2+"),
    "N4-": (0, 4, -1, None), "N3-": (0, 3, -1, "N4-"), "N2-": (0, 2, -1, "N3-"), "N1-": (0, 1, -1, "N2-"),
}
ORDER = (
    "F4+", "F3-", "N4-", "N3+", "F3+", "F2-", "N3-", "F0", "F2+", "F1-", "N2+", "N2-", "F1+", "N1+", "N1-",
)
FIRST = 4
TN = (((0,), (0,)), ((), ()))
NT = (((1,), (1,)), ((), ()))


def loop(count, step, start=0):
    def one(i, carry):
        step(i)
        return carry

    lax.fori_loop(start, count, one, 0)


def kernel(
    x_hbm, m_hbm, gin_hbm, head_hbm, w_hbm, sc_hbm, kg_ref, out_ref,
    xv, mv, wv, sv, gb, pg, bg, acc, xt, edge_i, edge, mh, sbuf, rbuf,
    ld_x, ld_m, ld_w, ld_s, ld_e,
    gm_send, gm_recv, ge_send, ge_recv, gd_send, gd_recv, hh_send,
    p0_send, p0_recv, mh_send, mh_recv, rs_send, rs_recv, ready,
):
    s = lax.axis_index("section")
    j = lax.axis_index("tile")
    z, y = j // RING, j % RING
    has_tile = (j > 0, j < TILES - 1)
    sends, takes = s > 0, s < SECTIONS - 1
    top = s == SECTIONS - 1
    last = T - 1

    def ring(distance, other=0):
        row = (z + other) % 2
        return row * RING + (y + distance + RING) % RING

    def beside(side):
        return j - 1 + 2 * side

    barrier = pltpu.get_barrier_semaphore()

    def greet(section, tile):
        pl.semaphore_signal(barrier, inc=1, device_id=(section, tile), device_id_type=MESH)

    for side in range(2):
        pl.when(has_tile[side])(lambda side=side: greet(s, beside(side)))
    greet(s, ring(1))
    greet(s, ring(-1))

    @pl.when(z == 0)
    def _():
        for distance in (-1, 0, 1):
            greet(s, ring(distance, 1))

    @pl.when(takes)
    def _():
        greet(s + 1, j)
        for side in range(2):
            pl.when(has_tile[side])(lambda side=side: greet(s + 1, beside(side)))

    def rows(i, count=1, lead=LEAD):
        return pl.ds((i + lead) * W, count * W)

    def local(src, dst, sem):
        return pltpu.make_async_copy(src, dst, sem)

    def to_tile(src, dst, send, recv, section, tile):
        return pltpu.make_async_remote_copy(
            src_ref=src, dst_ref=dst, send_sem=send, recv_sem=recv,
            device_id=(section, tile), device_id_type=MESH,
        )

    def edge_load(side):
        return local(
            m_hbm.at[pl.ds(1, T - 1), rows(side * (H - 2), 2, 0), :], edge_i.at[side], ld_e.at[side]
        )

    def first_load(h):
        return local(
            gin_hbm.at[rows(h * (H // 2), H // 2, 0)], gb.at[0, rows(h * (H // 2), H // 2)], gm_recv.at[0, h]
        )

    def mask_load(t):
        return local(m_hbm.at[t], mv.at[t], ld_m.at[t])

    def x_load(t):
        return local(x_hbm.at[t], xv.at[t], ld_x.at[t])

    w_load = local(w_hbm, wv, ld_w)
    s_load = local(sc_hbm, sv, ld_s)
    s_load.start()
    first_load(0).start()
    first_load(1).start()
    mask_load(0).start()
    edge_load(0).start()
    edge_load(1).start()
    w_load.start()
    x_load(0).start()
    for t in range(1, T):
        mask_load(t).start()
        x_load(t).start()

    inner = {0: ((1, 7), (8, 7)), 1: ((2, 5), (7, 7)), 2: ((1, 7), (8, 7))}
    ends = {0: (-1, H - 1), 1: (0, H - 2), 2: (-1, H - 1)}

    def pass_inner(t, h):
        first, count = inner[t][h]
        return to_tile(
            bg.at[t, rows(first, count, 1)], gb.at[t + 1, rows(first, count)],
            gm_send.at[t, h], gm_recv.at[t + 1, h], s - 1, j,
        )

    def pass_end(t, side):
        return to_tile(
            bg.at[t, rows(ends[t][side], 2, 1)], gb.at[t + 1, rows(ends[t][side], 2)],
            ge_send.at[t, side], ge_recv.at[t + 1, side], s - 1, j,
        )

    def far(t, side):
        return gb.at[t, rows(H - (H + 2) * side, 2)]

    def pass_aside(side):
        return to_tile(
            bg.at[1, rows(ends[1][side], 2, 1)], far(2, side),
            gd_send.at[side], gd_recv.at[1 - side], s - 1, beside(side),
        )

    def first_aside(side):
        return to_tile(
            pg.at[1, rows(side * (H - 2), 2)], far(0, side),
            p0_send.at[side], p0_recv.at[1 - side], s, beside(side),
        )

    def mask_aside(side):
        return to_tile(
            edge.at[side], mh.at[1 - side], mh_send.at[side], mh_recv.at[1 - side], s, beside(side)
        )

    def head_local(t, first, count, sem):
        return local(head_hbm.at[t, rows(first, count, 0)], gb.at[t + 1, rows(first, count)], sem)

    def head_aside(t, side):
        if t == 1:
            src, dst, recv = rows(side * (H - 2), 2, 0), far(2, side), gd_recv.at[1 - side]
        else:
            src, dst, recv = rows(side * (H - 1), 1, 0), gb.at[t + 1, rows(H - (H + 1) * side)], ge_recv.at[t + 1, 1 - side]
        return to_tile(head_hbm.at[t, src], dst, hh_send.at[t, side], recv, s, beside(side))

    @pl.when(top)
    def _():
        for t in range(T - 1):
            for h in range(2):
                head_local(t, *inner[t][h], gm_recv.at[t + 1, h]).start()
            for side in range(2):
                sem = ge_recv.at[t + 1, side]
                if t == 1:
                    head_local(t, ends[t][side], 2, sem).start()
                else:
                    head_local(t, side * (H - 1), 1, sem).start()

                    @pl.when(jnp.logical_not(has_tile[side]))
                    def _(t=t, side=side, sem=sem):
                        local(
                            head_hbm.at[t, rows(side * (H - 1), 1, 0)],
                            gb.at[t + 1, rows(side * (H + 1) - 1)], sem,
                        ).start()

    def put(t, row, value):
        count = value.shape[0]
        column = lax.broadcasted_iota(jnp.int32, (count, C), 0) % W
        dst = pl.ds((row + LEAD) * W, count)
        right = jnp.where(column == W - 1, 0.0, pltpu.roll(value, count - 1, 0))
        left = jnp.where(column == 0, 0.0, pltpu.roll(value, 1, 0))
        pg[3 * t, dst, :] = right.astype(BF16)
        pg[3 * t + 1, dst, :] = value.astype(BF16)
        pg[3 * t + 2, dst, :] = left.astype(BF16)

    s_load.wait()
    scales = sv[...]

    def own_rows(t, first, count):
        grads = gb[t, rows(first, count), :].astype(F32)
        put(t, first, jnp.where(mv[t, rows(first, count, 0), :] != 0, grads * scales, 0.0))

    depth = (2, 1, 2, 1)
    mask_at = (None, 0, 1, 3)

    def beyond(t, side):
        count = depth[t]
        first = H if side else -count

        @pl.when(has_tile[side])
        def _():
            grads = gb[t, rows(first, count), :].astype(F32)
            if t:
                grads = grads * mh[side, rows(mask_at[t], count, 0), :].astype(F32) * scales
            put(t, first, grads)

        @pl.when(jnp.logical_not(has_tile[side]))
        def _():
            for b in range(3):
                pg[3 * t + b, rows(first, count), :] = jnp.zeros((count * W, C), BF16)

    def conv(t, starts, count):
        total = None
        for a in range(3):
            for b in range(3):
                parts = [pg[3 * t + b, rows(i + 1 - a, count), :] for i in starts]
                term = lax.dot_general(
                    parts[0] if len(parts) == 1 else jnp.concatenate(parts, axis=0),
                    wv[(3 * a + b) * C : (3 * a + b + 1) * C, :],
                    NT, preferred_element_type=F32,
                )
                total = term if total is None else total + term
        return total.astype(BF16)

    def inner_part(t, h):
        first, count = inner[t][h]
        bg[t, rows(first, count, 1), :] = conv(t, [first], count)
        pl.when(sends)(lambda: pass_inner(t, h).start())

    def end_parts(t):
        both = conv(t, ends[t], 2)
        for side in range(2):
            bg[t, rows(ends[t][side], 2, 1), :] = both[side * 2 * W : (side + 1) * 2 * W]

        @pl.when(sends)
        def _():
            for side in range(2):
                if t == 1:
                    pl.when(has_tile[side])(lambda side=side: pass_aside(side).start())
            for side in range(2):
                pass_end(t, side).start()

    def kernel_term(t):
        def one(a):
            taps = pl.ds(pl.multiple_of((LEAD + 1 - a) * W, W), PX)
            for b in range(3):
                dst = pl.ds(pl.multiple_of((3 * a + b) * C, C), C)
                acc[dst, :] += lax.dot_general(
                    xv[t], pg[3 * t + b, taps, :], TN, preferred_element_type=F32
                )

        loop(3, one)

    def got_inner(t, h):
        first, count = inner[t - 1][h]
        local(head_hbm.at[0, rows(first, count, 0)], gb.at[t, rows(first, count)], gm_recv.at[t, h]).wait()

    def got_end(t, side):
        local(head_hbm.at[0, rows(0, 2, 0)], gb.at[t, rows(ends[t - 1][side], 2)], ge_recv.at[t, side]).wait()

    first_load(0).wait()
    first_load(1).wait()
    mask_load(0).wait()
    own_rows(0, 0, 8)
    own_rows(0, 8, 8)
    for side in range(2):
        edge_load(side).wait()
        pick = pl.ds(side * W, W)
        edge[side, 0:W, :] = edge_i[side, 0, pick, :].astype(BF16)
        edge[side, W : 3 * W, :] = edge_i[side, 1, :, :].astype(BF16)
        edge[side, 3 * W : 4 * W, :] = edge_i[side, 2, pick, :].astype(BF16)

    beside_count = has_tile[0].astype(jnp.int32) + has_tile[1].astype(jnp.int32)
    pl.semaphore_wait(barrier, 2 + 3 * z + beside_count + jnp.where(sends, beside_count + 1, 0))

    for side in range(2):
        pl.when(has_tile[side])(lambda side=side: first_aside(side).start())

    w_load.wait()
    inner_part(0, 0)
    inner_part(0, 1)

    @pl.when(z == 1)
    def _():
        for distance in (-1, 0, 1):
            pl.semaphore_signal(
                ready, inc=1, device_id=(s, ring(distance, 1)), device_id_type=MESH
            )

    for side in range(2):

        @pl.when(has_tile[side])
        def _(side=side):
            mask_aside(side).start()

            @pl.when(top)
            def _():
                for t in range(T - 1):
                    head_aside(t, side).start()


    def clear(i):
        acc[pl.ds(pl.multiple_of(i * C, C), C), :] = jnp.zeros((C, C), F32)

    loop(9, clear)
    for side in range(2):
        pl.when(has_tile[side])(
            lambda side=side: local(gin_hbm.at[rows(0, 2, 0)], far(0, 1 - side), p0_recv.at[side]).wait()
        )
        beyond(0, side)
    end_parts(0)

    mask_load(1).wait()
    got_inner(1, 0)
    own_rows(1, 1, 7)
    inner_part(1, 0)
    got_inner(1, 1)
    own_rows(1, 8, 7)
    inner_part(1, 1)
    x_load(0).wait()
    kernel_term(0)
    for side in range(2):
        pl.when(has_tile[side])(
            lambda side=side: local(edge.at[side], mh.at[side], mh_recv.at[side]).wait()
        )
        got_end(1, side)
        own_rows(1, side * (H - 1), 1)
        beyond(1, side)
    end_parts(1)
    x_load(1).wait()
    kernel_term(1)

    mask_load(2).wait()
    got_inner(2, 0)
    own_rows(2, 2, 5)
    got_inner(2, 1)
    own_rows(2, 7, 7)
    for side in range(2):
        got_end(2, side)
        own_rows(2, side * (H - 2), 2)
    inner_part(2, 0)
    inner_part(2, 1)
    for side in range(2):
        pl.when(has_tile[side])(
            lambda side=side: local(gin_hbm.at[rows(0, 2, 0)], far(2, 1 - side), gd_recv.at[side]).wait()
        )
        beyond(2, side)
    end_parts(2)
    x_load(2).wait()
    kernel_term(2)

    x_load(last).wait()
    turned = xv[last].T
    xt[0:C, :] = turned
    xt[C : 2 * C, :] = turned
    mask_load(last).wait()
    got_inner(last, 0)
    own_rows(last, 1, 7)
    got_inner(last, 1)
    own_rows(last, 8, 7)
    for side in range(2):
        got_end(last, side)
        own_rows(last, side * (H - 1), 1)
        beyond(last, side)

    def block_row(name):
        kind, away, way, _ = PLAN[name]
        return ring(way * away, kind) * ROWS

    def piece(name, part, whole=False):
        start, count = (0, ROWS) if whole else PIECES[part]
        return pl.ds(pl.multiple_of(block_row(name) + start, 16), count)

    def message(name, part):
        kind, away, way, _ = PLAN[name]
        i = ORDER.index(name)
        at = pl.ds(*PIECES[part])
        crosses = kind == 1 and away <= 1
        return to_tile(
            sbuf.at[i, at], rbuf.at[i, at], rs_send.at[i, part], rs_recv.at[i, part],
            s, ring(way, 1 if crosses else 0),
        )

    def first_message(name):
        row0 = block_row(name)
        tap = row0 // C
        at = pl.multiple_of(row0 - tap * C, 16)
        lhs = xt[pl.ds(at, ROWS), :]

        def term(tap):
            a, b = tap // 3, tap % 3
            taps = pl.ds(pl.multiple_of((LEAD + 1 - a) * W, W), PX)
            return jnp.dot(lhs, pg[3 * last + b, taps, :], preferred_element_type=F32)

        row = lax.broadcasted_iota(jnp.int32, (ROWS, C), 0) + at
        own = jnp.where(row < C, term(tap), term(jnp.minimum(tap + 1, 8)))
        sbuf[ORDER.index(name)] = (acc[piece(name, 0, True), :] + own).astype(BF16)
        for part in range(2):
            message(name, part).start()

    def later_message(name, part):
        total = acc[piece(name, part), :]
        before = PLAN[name][3]
        at = pl.ds(*PIECES[part])
        if before:
            message(before, part).wait_recv()
            total = total + rbuf[ORDER.index(before), at, :].astype(F32)
        sbuf[ORDER.index(name), at, :] = total.astype(BF16)
        message(name, part).start()

    for name in ORDER[:FIRST]:
        first_message(name)
    kernel_term(last)
    for name in ORDER[FIRST:]:
        if name == "F0":
            pl.when(z == 0)(lambda: pl.semaphore_wait(ready, 3))
        for part in range(2):
            later_message(name, part)
        if name == "F1+":
            out_ref[...] = conv(last, [0], H)

    for part in range(2):
        start, count = PIECES[part]
        at = pl.ds(start, count)
        total = acc[pl.ds(pl.multiple_of(j * ROWS + start, 16), count), :]
        for name in ("F0", "F1-", "N1+", "F1+", "N1-"):
            message(name, part).wait_recv()
            total = total + rbuf[ORDER.index(name), at, :].astype(F32)
        kg_ref[at, :] = total * (1.0 / math.sqrt(T * TILES * PX))

    for name in ORDER:
        for part in range(2):
            message(name, part).wait_send()
    for side in range(2):

        @pl.when(has_tile[side])
        def _(side=side):
            first_aside(side).wait_send()
            mask_aside(side).wait_send()
            pl.when(sends)(lambda: pass_aside(side).wait_send())

            @pl.when(top)
            def _():
                for t in range(T - 1):
                    head_aside(t, side).wait_send()

    @pl.when(sends)
    def _():
        for t in range(T - 1):
            for k in range(2):
                pass_inner(t, k).wait_send()
                pass_end(t, k).wait_send()


def store(kg_in, out_in, kg_hbm, out_hbm, kg_sem, out_sem):
    copies = (
        pltpu.make_async_copy(kg_in, kg_hbm, kg_sem),
        pltpu.make_async_copy(out_in, out_hbm, out_sem),
    )
    for copy in copies:
        copy.start()
    for copy in copies:
        copy.wait()


def per_device(saved_inputs, relu_mask, grads_in, head_grads, kernels, bn_scale):
    any_space = pl.BlockSpec(memory_space=pl.ANY)
    vmem = pl.BlockSpec(memory_space=pltpu.VMEM)
    dma = pltpu.SemaphoreType.DMA
    kernel_grads, outgoing = pl.pallas_call(
        kernel,
        out_shape=(
            pltpu.VMEM((ROWS, C), F32),
            pltpu.VMEM((PX, C), BF16),
        ),
        in_specs=[any_space] * 6,
        out_specs=(vmem, vmem),
        scratch_shapes=[
            pltpu.VMEM((T, PX, C), BF16),
            pltpu.VMEM((T, PX, C), jnp.int32),
            pltpu.VMEM((9 * C, C), BF16),
            pltpu.VMEM((1, C), F32),
            pltpu.VMEM((T, GRID, C), BF16),
            pltpu.VMEM((3 * T, GRID, C), BF16),
            pltpu.VMEM((T - 1, PX + 2 * W, C), BF16),
            pltpu.VMEM((9 * C, C), F32),
            pltpu.VMEM((2 * C, PX), BF16),
            pltpu.VMEM((2, T - 1, 2 * W, C), jnp.int32),
            pltpu.VMEM((2, 4 * W, C), BF16),
            pltpu.VMEM((2, 4 * W, C), BF16),
            pltpu.VMEM((len(ORDER), ROWS, C), BF16),
            pltpu.VMEM((len(ORDER), ROWS, C), BF16),
            dma((T,)),
            dma((T,)),
            dma,
            dma,
            dma((2,)),
            dma((T - 1, 2)),
            dma((T, 2)),
            dma((T - 1, 2)),
            dma((T, 2)),
            dma((2,)),
            dma((2,)),
            dma((T - 1, 2)),
            dma((2,)),
            dma((2,)),
            dma((2,)),
            dma((2,)),
            dma((len(ORDER), 2)),
            dma((len(ORDER), 2)),
            pltpu.SemaphoreType.REGULAR,
        ],
        compiler_params=pltpu.CompilerParams(
            collective_id=0, has_side_effects=True, vmem_limit_bytes=62 * 2**20
        ),
        cost_estimate=pl.CostEstimate(
            flops=4 * T * PX * 9 * C * C, bytes_accessed=6 * 2**20, transcendentals=0
        ),
    )(
        saved_inputs.reshape(T, PX, C),
        relu_mask.reshape(T, PX, C),
        grads_in.reshape(PX, C),
        head_grads.reshape(T - 1, PX, C),
        kernels.reshape(9 * C, C),
        bn_scale,
    )
    kernel_grads, outgoing = pl.pallas_call(
        store,
        out_shape=(
            jax.ShapeDtypeStruct((ROWS, C), F32),
            jax.ShapeDtypeStruct((PX, C), BF16),
        ),
        in_specs=[vmem] * 2,
        out_specs=(pl.BlockSpec(memory_space=pltpu.HBM),) * 2,
        scratch_shapes=[dma, dma],
        compiler_params=pltpu.CompilerParams(vmem_limit_bytes=2**20),
    )(kernel_grads, outgoing)
    return kernel_grads[None], outgoing.reshape(1, H, W, C)


def solution(mesh):
    return jax.shard_map(
        per_device,
        mesh=mesh,
        in_specs=(
            P("section", None, "tile", None, None),
            P("section", None, "tile", None, None),
            P("section", "tile", None, None),
            P(None, "tile", None, None),
            P("section", None, None, None, None),
            P("section", None),
        ),
        out_specs=(P("section", "tile", None), P("section", "tile", None, None)),
        check_vma=False,
    )
```

```python
import functools
import math

import jax
import jax.numpy as jnp
from jax import lax
from jax.experimental import pallas as pl
from jax.experimental.pallas import tpu as pltpu
from jax.sharding import PartitionSpec as P

MESH = pl.DeviceIdType.MESH
F32 = jnp.float32
BF16 = jnp.bfloat16
T, H, W, C = 4, 16, 32, 256
PX = H * W
LEAD = 2
GRID = PX + 2 * LEAD * W
SECTIONS, TILES, RING = 32, 16, 8
ROWS = 9 * C // TILES
PIECES = ((0, ROWS),)
PLAN = {
    "F4+": (1, 4, 1, None), "F3+": (1, 3, 1, "F4+"), "F2+": (1, 2, 1, "F3+"), "F1+": (1, 1, 1, "F2+"),
    "F3-": (1, 3, -1, None), "F2-": (1, 2, -1, "F3-"), "F1-": (1, 1, -1, "F2-"), "F0": (1, 0, 0, None),
    "N3+": (0, 3, 1, None), "N2+": (0, 2, 1, "N3+"), "N1+": (0, 1, 1, "N2+"),
    "N4-": (0, 4, -1, None), "N3-": (0, 3, -1, "N4-"), "N2-": (0, 2, -1, "N3-"), "N1-": (0, 1, -1, "N2-"),
}
ORDER = (
    "F4+", "F3-", "N4-", "N3+", "F3+", "F2-", "N3-", "F0", "F2+", "F1-", "N2+", "N2-", "F1+", "N1+", "N1-",
)
FIRST = 4
TN = (((0,), (0,)), ((), ()))
NT = (((1,), (1,)), ((), ()))


def loop(count, step, start=0):
    def one(i, carry):
        step(i)
        return carry

    lax.fori_loop(start, count, one, 0)


def kernel(
    x_hbm, m_hbm, gin_hbm, head_hbm, w_hbm, sc_hbm, kg_ref, out_ref,
    xv, mv, wv, sv, gb, pg, bg, acc, xt, edge_i, edge, mh, sbuf, rbuf,
    ld_x, ld_m, ld_w, ld_s, ld_e,
    gm_send, gm_recv, ge_send, ge_recv, gd_send, gd_recv, hh_send,
    p0_send, p0_recv, mh_send, mh_recv, rs_send, rs_recv, ready,
):
    s = lax.axis_index("section")
    j = lax.axis_index("tile")
    z, y = j // RING, j % RING
    has_tile = (j > 0, j < TILES - 1)
    sends, takes = s > 0, s < SECTIONS - 1
    top = s == SECTIONS - 1
    last = T - 1

    def ring(distance, other=0):
        row = (z + other) % 2
        return row * RING + (y + distance + RING) % RING

    def beside(side):
        return j - 1 + 2 * side

    barrier = pltpu.get_barrier_semaphore()

    def greet(section, tile):
        pl.semaphore_signal(barrier, inc=1, device_id=(section, tile), device_id_type=MESH)

    for side in range(2):
        pl.when(has_tile[side])(lambda side=side: greet(s, beside(side)))
    greet(s, ring(1))
    greet(s, ring(-1))

    @pl.when(z == 0)
    def _():
        for distance in (-1, 0, 1):
            greet(s, ring(distance, 1))

    @pl.when(takes)
    def _():
        greet(s + 1, j)
        for side in range(2):
            pl.when(has_tile[side])(lambda side=side: greet(s + 1, beside(side)))

    def rows(i, count=1, lead=LEAD):
        return pl.ds((i + lead) * W, count * W)

    def local(src, dst, sem):
        return pltpu.make_async_copy(src, dst, sem)

    def to_tile(src, dst, send, recv, section, tile):
        return pltpu.make_async_remote_copy(
            src_ref=src, dst_ref=dst, send_sem=send, recv_sem=recv,
            device_id=(section, tile), device_id_type=MESH,
        )

    def edge_load(side):
        return local(
            m_hbm.at[pl.ds(1, T - 1), rows(side * (H - 2), 2, 0), :], edge_i.at[side], ld_e.at[side]
        )

    def first_load(h):
        return local(
            gin_hbm.at[rows(h * (H // 2), H // 2, 0)], gb.at[0, rows(h * (H // 2), H // 2)], gm_recv.at[0, h]
        )

    def mask_load(t):
        return local(m_hbm.at[t], mv.at[t], ld_m.at[t])

    def x_load(t):
        return local(x_hbm.at[t], xv.at[t], ld_x.at[t])

    w_load = local(w_hbm, wv, ld_w)
    s_load = local(sc_hbm, sv, ld_s)
    s_load.start()
    first_load(0).start()
    first_load(1).start()
    mask_load(0).start()
    edge_load(0).start()
    edge_load(1).start()
    w_load.start()
    x_load(0).start()
    for t in range(1, T):
        mask_load(t).start()
        x_load(t).start()

    inner = {0: ((1, 7), (8, 7)), 1: ((2, 5), (7, 7)), 2: ((1, 7), (8, 7))}
    ends = {0: (-1, H - 1), 1: (0, H - 2), 2: (-1, H - 1)}

    def pass_inner(t, h):
        first, count = inner[t][h]
        return to_tile(
            bg.at[t, rows(first, count, 1)], gb.at[t + 1, rows(first, count)],
            gm_send.at[t, h], gm_recv.at[t + 1, h], s - 1, j,
        )

    def pass_end(t, side):
        return to_tile(
            bg.at[t, rows(ends[t][side], 2, 1)], gb.at[t + 1, rows(ends[t][side], 2)],
            ge_send.at[t, side], ge_recv.at[t + 1, side], s - 1, j,
        )

    def far(t, side):
        return gb.at[t, rows(H - (H + 2) * side, 2)]

    def pass_aside(side):
        return to_tile(
            bg.at[1, rows(ends[1][side], 2, 1)], far(2, side),
            gd_send.at[side], gd_recv.at[1 - side], s - 1, beside(side),
        )

    def first_aside(side):
        return to_tile(
            pg.at[1, rows(side * (H - 2), 2)], far(0, side),
            p0_send.at[side], p0_recv.at[1 - side], s, beside(side),
        )

    depth = (2, 1, 2, 1)
    mask_at = (None, 0, 1, 3)

    def mask_aside(t, side):
        at = rows(mask_at[t], depth[t], 0)
        return to_tile(
            edge.at[side, at], mh.at[1 - side, at],
            mh_send.at[t - 1, side], mh_recv.at[t - 1, 1 - side], s, beside(side),
        )

    def got_mask(t, side):
        at = rows(mask_at[t], depth[t], 0)
        pl.when(has_tile[side])(
            lambda: local(edge.at[side, at], mh.at[side, at], mh_recv.at[t - 1, side]).wait()
        )

    def head_local(t, first, count, sem):
        return local(head_hbm.at[t, rows(first, count, 0)], gb.at[t + 1, rows(first, count)], sem)

    def head_aside(t, side):
        if t == 1:
            src, dst, recv = rows(side * (H - 2), 2, 0), far(2, side), gd_recv.at[1 - side]
        else:
            src, dst, recv = rows(side * (H - 1), 1, 0), gb.at[t + 1, rows(H - (H + 1) * side)], ge_recv.at[t + 1, 1 - side]
        return to_tile(head_hbm.at[t, src], dst, hh_send.at[t, side], recv, s, beside(side))

    @pl.when(top)
    def _():
        for t in range(T - 1):
            for h in range(2):
                head_local(t, *inner[t][h], gm_recv.at[t + 1, h]).start()
            for side in range(2):
                sem = ge_recv.at[t + 1, side]
                if t == 1:
                    head_local(t, ends[t][side], 2, sem).start()
                else:
                    head_local(t, side * (H - 1), 1, sem).start()

                    @pl.when(jnp.logical_not(has_tile[side]))
                    def _(t=t, side=side, sem=sem):
                        local(
                            head_hbm.at[t, rows(side * (H - 1), 1, 0)],
                            gb.at[t + 1, rows(side * (H + 1) - 1)], sem,
                        ).start()

    def put(t, row, value):
        count = value.shape[0]
        column = lax.broadcasted_iota(jnp.int32, (count, C), 0) % W
        dst = pl.ds((row + LEAD) * W, count)
        right = jnp.where(column == W - 1, 0.0, pltpu.roll(value, count - 1, 0))
        left = jnp.where(column == 0, 0.0, pltpu.roll(value, 1, 0))
        pg[3 * t, dst, :] = right.astype(BF16)
        pg[3 * t + 1, dst, :] = value.astype(BF16)
        pg[3 * t + 2, dst, :] = left.astype(BF16)

    s_load.wait()
    scales = sv[...]

    def own_rows(t, first, count):
        grads = gb[t, rows(first, count), :].astype(F32)
        put(t, first, jnp.where(mv[t, rows(first, count, 0), :] != 0, grads * scales, 0.0))

    def beyond(t, side):
        count = depth[t]
        first = H if side else -count

        @pl.when(has_tile[side])
        def _():
            grads = gb[t, rows(first, count), :].astype(F32)
            if t:
                grads = grads * mh[side, rows(mask_at[t], count, 0), :].astype(F32) * scales
            put(t, first, grads)

        @pl.when(jnp.logical_not(has_tile[side]))
        def _():
            for b in range(3):
                pg[3 * t + b, rows(first, count), :] = jnp.zeros((count * W, C), BF16)

    def conv(t, starts, count):
        total = None
        for a in range(3):
            for b in range(3):
                parts = [pg[3 * t + b, rows(i + 1 - a, count), :] for i in starts]
                term = lax.dot_general(
                    parts[0] if len(parts) == 1 else jnp.concatenate(parts, axis=0),
                    wv[(3 * a + b) * C : (3 * a + b + 1) * C, :],
                    NT, preferred_element_type=F32,
                )
                total = term if total is None else total + term
        return total.astype(BF16)

    def inner_part(t, h):
        first, count = inner[t][h]
        bg[t, rows(first, count, 1), :] = conv(t, [first], count)
        pl.when(sends)(lambda: pass_inner(t, h).start())

    def end_parts(t):
        both = conv(t, ends[t], 2)
        for side in range(2):
            bg[t, rows(ends[t][side], 2, 1), :] = both[side * 2 * W : (side + 1) * 2 * W]

        @pl.when(sends)
        def _():
            for side in range(2):
                if t == 1:
                    pl.when(has_tile[side])(lambda side=side: pass_aside(side).start())
            for side in range(2):
                pass_end(t, side).start()

    def kernel_term(t):
        def one(a):
            taps = pl.ds(pl.multiple_of((LEAD + 1 - a) * W, W), PX)
            for b in range(3):
                dst = pl.ds(pl.multiple_of((3 * a + b) * C, C), C)
                acc[dst, :] += lax.dot_general(
                    xv[t], pg[3 * t + b, taps, :], TN, preferred_element_type=F32
                )

        loop(3, one)

    def got_inner(t, h):
        first, count = inner[t - 1][h]
        local(head_hbm.at[0, rows(first, count, 0)], gb.at[t, rows(first, count)], gm_recv.at[t, h]).wait()

    def got_end(t, side):
        local(head_hbm.at[0, rows(0, 2, 0)], gb.at[t, rows(ends[t - 1][side], 2)], ge_recv.at[t, side]).wait()

    first_load(0).wait()
    first_load(1).wait()
    mask_load(0).wait()
    own_rows(0, 0, 8)
    own_rows(0, 8, 8)
    for side in range(2):
        edge_load(side).wait()
        pick = pl.ds(side * W, W)
        edge[side, 0:W, :] = edge_i[side, 0, pick, :].astype(BF16)
        edge[side, W : 3 * W, :] = edge_i[side, 1, :, :].astype(BF16)
        edge[side, 3 * W : 4 * W, :] = edge_i[side, 2, pick, :].astype(BF16)

    beside_count = has_tile[0].astype(jnp.int32) + has_tile[1].astype(jnp.int32)
    pl.semaphore_wait(barrier, 2 + 3 * z + beside_count + jnp.where(sends, beside_count + 1, 0))

    for side in range(2):
        pl.when(has_tile[side])(lambda side=side: first_aside(side).start())

    w_load.wait()
    inner_part(0, 0)
    inner_part(0, 1)

    @pl.when(z == 1)
    def _():
        for distance in (-1, 0, 1):
            pl.semaphore_signal(
                ready, inc=1, device_id=(s, ring(distance, 1)), device_id_type=MESH
            )

    for side in range(2):

        @pl.when(has_tile[side])
        def _(side=side):
            for t in range(1, T):
                mask_aside(t, side).start()

            @pl.when(top)
            def _():
                for t in range(T - 1):
                    head_aside(t, side).start()


    def clear(i):
        acc[pl.ds(pl.multiple_of(i * C, C), C), :] = jnp.zeros((C, C), F32)

    loop(9, clear)
    for side in range(2):
        pl.when(has_tile[side])(
            lambda side=side: local(gin_hbm.at[rows(0, 2, 0)], far(0, 1 - side), p0_recv.at[side]).wait()
        )
        beyond(0, side)
    end_parts(0)

    mask_load(1).wait()
    got_inner(1, 0)
    own_rows(1, 1, 7)
    inner_part(1, 0)
    got_inner(1, 1)
    own_rows(1, 8, 7)
    inner_part(1, 1)
    x_load(0).wait()
    kernel_term(0)
    for side in range(2):
        got_end(1, side)
        got_mask(1, side)
        own_rows(1, side * (H - 1), 1)
        beyond(1, side)
    end_parts(1)
    x_load(1).wait()
    kernel_term(1)

    mask_load(2).wait()
    got_inner(2, 0)
    own_rows(2, 2, 5)
    got_inner(2, 1)
    own_rows(2, 7, 7)
    for side in range(2):
        got_end(2, side)
        own_rows(2, side * (H - 2), 2)
    inner_part(2, 0)
    inner_part(2, 1)
    for side in range(2):
        pl.when(has_tile[side])(
            lambda side=side: local(gin_hbm.at[rows(0, 2, 0)], far(2, 1 - side), gd_recv.at[side]).wait()
        )
        got_mask(2, side)
        beyond(2, side)
    end_parts(2)
    x_load(2).wait()
    kernel_term(2)

    x_load(last).wait()
    turned = xv[last].T
    xt[0:C, :] = turned
    xt[C : 2 * C, :] = turned
    mask_load(last).wait()
    got_inner(last, 0)
    own_rows(last, 1, 7)
    got_inner(last, 1)
    own_rows(last, 8, 7)
    for side in range(2):
        got_end(last, side)
        got_mask(last, side)
        own_rows(last, side * (H - 1), 1)
        beyond(last, side)

    def block_row(name):
        kind, away, way, _ = PLAN[name]
        return ring(way * away, kind) * ROWS

    def piece(name, part, whole=False):
        start, count = (0, ROWS) if whole else PIECES[part]
        return pl.ds(pl.multiple_of(block_row(name) + start, 16), count)

    def message(name, part):
        kind, away, way, _ = PLAN[name]
        i = ORDER.index(name)
        at = pl.ds(*PIECES[part])
        crosses = kind == 1 and away <= 1
        return to_tile(
            sbuf.at[i, at], rbuf.at[i, at], rs_send.at[i, part], rs_recv.at[i, part],
            s, ring(way, 1 if crosses else 0),
        )

    def first_message(name):
        row0 = block_row(name)
        tap = row0 // C
        at = pl.multiple_of(row0 - tap * C, 16)
        lhs = xt[pl.ds(at, ROWS), :]

        def term(tap):
            a, b = tap // 3, tap % 3
            taps = pl.ds(pl.multiple_of((LEAD + 1 - a) * W, W), PX)
            return jnp.dot(lhs, pg[3 * last + b, taps, :], preferred_element_type=F32)

        row = lax.broadcasted_iota(jnp.int32, (ROWS, C), 0) + at
        own = jnp.where(row < C, term(tap), term(jnp.minimum(tap + 1, 8)))
        sbuf[ORDER.index(name)] = (acc[piece(name, 0, True), :] + own).astype(BF16)
        for part in range(len(PIECES)):
            message(name, part).start()

    def later_message(name, part):
        total = acc[piece(name, part), :]
        before = PLAN[name][3]
        at = pl.ds(*PIECES[part])
        if before:
            message(before, part).wait_recv()
            total = total + rbuf[ORDER.index(before), at, :].astype(F32)
        sbuf[ORDER.index(name), at, :] = total.astype(BF16)
        message(name, part).start()

    for name in ORDER[:FIRST]:
        first_message(name)
    kernel_term(last)
    for name in ORDER[FIRST:]:
        if name == "F0":
            pl.when(z == 0)(lambda: pl.semaphore_wait(ready, 3))
        for part in range(len(PIECES)):
            later_message(name, part)
        if name == "F1+":
            out_ref[...] = conv(last, [0], H)

    for part in range(len(PIECES)):
        start, count = PIECES[part]
        at = pl.ds(start, count)
        total = acc[pl.ds(pl.multiple_of(j * ROWS + start, 16), count), :]
        for name in ("F0", "F1-", "N1+", "F1+", "N1-"):
            message(name, part).wait_recv()
            total = total + rbuf[ORDER.index(name), at, :].astype(F32)
        kg_ref[at, :] = total * (1.0 / math.sqrt(T * TILES * PX))

    for name in ORDER:
        for part in range(len(PIECES)):
            message(name, part).wait_send()
    for side in range(2):

        @pl.when(has_tile[side])
        def _(side=side):
            first_aside(side).wait_send()
            for t in range(1, T):
                mask_aside(t, side).wait_send()
            pl.when(sends)(lambda: pass_aside(side).wait_send())

            @pl.when(top)
            def _():
                for t in range(T - 1):
                    head_aside(t, side).wait_send()

    @pl.when(sends)
    def _():
        for t in range(T - 1):
            for k in range(2):
                pass_inner(t, k).wait_send()
                pass_end(t, k).wait_send()


def store(kg_in, out_in, kg_hbm, out_hbm, kg_sem, out_sem):
    copies = (
        pltpu.make_async_copy(kg_in, kg_hbm, kg_sem),
        pltpu.make_async_copy(out_in, out_hbm, out_sem),
    )
    for copy in copies:
        copy.start()
    for copy in copies:
        copy.wait()


def per_device(saved_inputs, relu_mask, grads_in, head_grads, kernels, bn_scale):
    any_space = pl.BlockSpec(memory_space=pl.ANY)
    vmem = pl.BlockSpec(memory_space=pltpu.VMEM)
    dma = pltpu.SemaphoreType.DMA
    kernel_grads, outgoing = pl.pallas_call(
        kernel,
        out_shape=(
            pltpu.VMEM((ROWS, C), F32),
            pltpu.VMEM((PX, C), BF16),
        ),
        in_specs=[any_space] * 6,
        out_specs=(vmem, vmem),
        scratch_shapes=[
            pltpu.VMEM((T, PX, C), BF16),
            pltpu.VMEM((T, PX, C), jnp.int32),
            pltpu.VMEM((9 * C, C), BF16),
            pltpu.VMEM((1, C), F32),
            pltpu.VMEM((T, GRID, C), BF16),
            pltpu.VMEM((3 * T, GRID, C), BF16),
            pltpu.VMEM((T - 1, PX + 2 * W, C), BF16),
            pltpu.VMEM((9 * C, C), F32),
            pltpu.VMEM((2 * C, PX), BF16),
            pltpu.VMEM((2, T - 1, 2 * W, C), jnp.int32),
            pltpu.VMEM((2, 4 * W, C), BF16),
            pltpu.VMEM((2, 4 * W, C), BF16),
            pltpu.VMEM((len(ORDER), ROWS, C), BF16),
            pltpu.VMEM((len(ORDER), ROWS, C), BF16),
            dma((T,)),
            dma((T,)),
            dma,
            dma,
            dma((2,)),
            dma((T - 1, 2)),
            dma((T, 2)),
            dma((T - 1, 2)),
            dma((T, 2)),
            dma((2,)),
            dma((2,)),
            dma((T - 1, 2)),
            dma((2,)),
            dma((2,)),
            dma((T - 1, 2)),
            dma((T - 1, 2)),
            dma((len(ORDER), len(PIECES))),
            dma((len(ORDER), len(PIECES))),
            pltpu.SemaphoreType.REGULAR,
        ],
        compiler_params=pltpu.CompilerParams(
            collective_id=0, has_side_effects=True, vmem_limit_bytes=62 * 2**20
        ),
        cost_estimate=pl.CostEstimate(
            flops=4 * T * PX * 9 * C * C, bytes_accessed=6 * 2**20, transcendentals=0
        ),
    )(
        saved_inputs.reshape(T, PX, C),
        relu_mask.reshape(T, PX, C),
        grads_in.reshape(PX, C),
        head_grads.reshape(T - 1, PX, C),
        kernels.reshape(9 * C, C),
        bn_scale,
    )
    kernel_grads, outgoing = pl.pallas_call(
        store,
        out_shape=(
            jax.ShapeDtypeStruct((ROWS, C), F32),
            jax.ShapeDtypeStruct((PX, C), BF16),
        ),
        in_specs=[vmem] * 2,
        out_specs=(pl.BlockSpec(memory_space=pltpu.HBM),) * 2,
        scratch_shapes=[dma, dma],
        compiler_params=pltpu.CompilerParams(vmem_limit_bytes=2**20),
    )(kernel_grads, outgoing)
    return kernel_grads[None], outgoing.reshape(1, H, W, C)


def solution(mesh):
    return jax.shard_map(
        per_device,
        mesh=mesh,
        in_specs=(
            P("section", None, "tile", None, None),
            P("section", None, "tile", None, None),
            P("section", "tile", None, None),
            P(None, "tile", None, None),
            P("section", None, None, None, None),
            P("section", None),
        ),
        out_specs=(P("section", "tile", None), P("section", "tile", None, None)),
        check_vma=False,
    )
```
